256 devices in a mesh: term: 64 (over z, x, core), sector: 4 (over y).
Axes of the slice: x: 4, y: 4, z: 8, core: 2. Of those that a mesh axis runs over, the one named last changes fastest.
Arguments:
- psi_start: float32 [4, 384, 384], P('sector'), may hold values from -6 to 6
- diagonal: float32 [4, 384, 384], P('sector'), may hold values from -3 to 3
- left_ops: float32 [1024, 384, 384], P(('term', 'sector')), may hold values from -0.3125 to 0.3125
- right_ops: float32 [1024, 384, 384], P(('term', 'sector')), may hold values from -0.02734375 to 0.02734375
- pair_in: int32 [256, 4], P(('term', 'sector')), may hold values from 0 to 3
- pair_out: int32 [256, 4], P(('term', 'sector')), may hold values from 0 to 3
- pair_count: int32 [256], P(('term', 'sector')), may hold values from 1 to 4, as said below
Outputs:
- psi_final: float32 [4, 384, 384], P('sector')
- energies: float32 [2], replicated
The draws below stay inside these ranges and needn't reach their ends.
Inputs may be any that keep to these rules, and one draw needn't show every extreme that they name: `pair_count`: some device has all 4 slots live in every draw.
All inputs are finite; a program needn't handle non-finite values.
Results may differ from the reference program's by a relative error of at most 0.00013.
Values sent between devices are 32-bit elements; how exact they have to be, the bound alone decides.
A program may use at most 64 MiB of HBM per device.

```python
import jax
import jax.numpy as jnp
from jax import lax

B = 384
PAIRS = 4
ITERS = 2
SECTORS = 4
TERMS_SEC = 256
DEVICES = 256


def draw_pair_count(key, part):
    first_key, second_key = jax.random.split(jax.random.fold_in(key, 17))
    counts = jax.random.randint(first_key, (DEVICES,), 1, PAIRS + 1)
    chosen = jax.random.randint(second_key, (), 0, DEVICES)
    return jnp.where(jnp.arange(DEVICES) == chosen, PAIRS, counts).astype(jnp.int32)


def with_ends(drawn, stream_key, least, high):
    longest = drawn.shape.index(max(drawn.shape))
    spots = []
    for shift in (0, 1):
        where = [jax.random.randint(jax.random.fold_in(stream_key, axis), (), 0, length) for axis, length in enumerate(drawn.shape)]
        where[longest] = (where[longest] + shift) % drawn.shape[longest]
        spots.append(tuple(where))
    return drawn.at[spots[0]].set(least).at[spots[1]].set(high)


def level_of(rng, dims, cuts, low, largest):
    gain, own = 1.0, jax.random.fold_in(rng, 6)
    for position, parts in cuts:
        draws = jnp.exp(jax.random.uniform(jax.random.fold_in(own, position), (parts,), jnp.float32, low / len(cuts), largest / len(cuts)))
        gain = gain * jnp.repeat(draws, dims[position] // parts).reshape([-1 if axis == position else 1 for axis in range(len(dims))])
    return gain


def scatter_about(own_key, extent, deviation, most, shards=(), kind=jnp.bfloat16):
    values = deviation * jax.random.normal(own_key, extent, jnp.float32)
    if shards:
        values = values * level_of(own_key, extent, shards, -0.22, 0.18)
    return jnp.clip(values, -most, most).astype(kind)


def setup_inputs(seed: int = 0) -> dict:
    key_of = jax.random.split(jax.random.key(seed), 8)
    return {
        "psi_start": scatter_about(key_of[0], (SECTORS, B, B), 1.0, 6.0, ((0, 4),), jnp.float32),
        "diagonal": jnp.clip(jax.random.uniform(key_of[1], (SECTORS, B, B), jnp.float32, -3.0, 3.0) * level_of(key_of[1], (SECTORS, B, B), ((0, 4),), -0.4, 0.0), -3.0, 3.0),
        "left_ops": scatter_about(key_of[2], (DEVICES * PAIRS, B, B), B ** -0.5, 0.3125, ((0, 256),), jnp.float32),
        "right_ops": scatter_about(key_of[3], (DEVICES * PAIRS, B, B), (B * TERMS_SEC // 2) ** -0.5, 0.02734375, ((0, 256),), jnp.float32),
        "pair_in": with_ends(jax.random.randint(key_of[4], (DEVICES, PAIRS), 0, SECTORS), jax.random.fold_in(key_of[4], 1), 0, SECTORS - 1).astype(jnp.int32),
        "pair_out": with_ends(jax.random.randint(key_of[5], (DEVICES, PAIRS), 0, SECTORS), jax.random.fold_in(key_of[5], 1), 0, SECTORS - 1).astype(jnp.int32),
        "pair_count": draw_pair_count(jax.random.fold_in(key_of[7], 71), 0),
    }


epsilon = 1e-06

def reference(psi_start, diagonal, left_ops, right_ops, pair_in, pair_out, pair_count):
    flat_in = pair_in.reshape(-1).astype(jnp.int32)
    flat_out = pair_out.reshape(-1).astype(jnp.int32)
    slot_ids = jnp.arange(flat_in.shape[0], dtype=jnp.int32)
    live = (slot_ids % PAIRS < jnp.repeat(pair_count, PAIRS)).astype(jnp.float32)

    def apply_all(vector):

        def one_pair(pair_slot, partial_value):
            source = lax.dynamic_index_in_dim(vector, flat_in[pair_slot], 0, keepdims=False)
            left_block = lax.dynamic_index_in_dim(left_ops, pair_slot, 0, keepdims=False)
            right_block = lax.dynamic_index_in_dim(right_ops, pair_slot, 0, keepdims=False)
            inner_prod = jnp.dot(left_block, source, precision=lax.Precision.HIGHEST)
            product = lax.dot_general(inner_prod, right_block, (((1,), (1,)), ((), ())), precision=lax.Precision.HIGHEST)
            product = product * live[pair_slot]
            target = flat_out[pair_slot]
            current = lax.dynamic_index_in_dim(partial_value, target, 0, keepdims=False)
            return lax.dynamic_update_index_in_dim(partial_value, current + product, target, 0)
        return lax.fori_loop(0, flat_in.shape[0], one_pair, jnp.zeros_like(vector))
    vector = psi_start
    energies = []
    for sweep in range(ITERS):
        mean_square = jnp.mean(vector * vector) + epsilon
        normed = vector / jnp.sqrt(mean_square)
        sigma = apply_all(normed)
        rayleigh = jnp.mean(normed * sigma)
        residual = sigma - rayleigh * normed
        correction = residual / jnp.maximum(jnp.abs(diagonal - rayleigh), 1.0)
        vector = normed - correction
        energies.append(rayleigh)
    return (vector, jnp.stack(energies))
```

```python
import functools

import jax
import jax.numpy as jnp
from jax import lax
from jax.experimental import pallas as pl
from jax.experimental.pallas import tpu as pltpu
from jax.sharding import PartitionSpec as P

STEPS = 2
EPSILON = 1e-06
N = 384
CELLS = float(4 * N * N)
F32 = jnp.float32
BF16 = jnp.bfloat16


def matmul(a, b):
    return lax.dot_general(a, b, (((1,), (0,)), ((), ())), preferred_element_type=F32)


def halves(value):
    high = value.astype(BF16)
    return high, (value - high.astype(F32)).astype(BF16)


def kernel(
    pair_in,
    pair_out,
    pair_count,
    psi,
    diagonal,
    left_hbm,
    right_hbm,
    out,
    energies,
    left,
    right,
    left3,
    right3,
    vec3,
    inner3,
    product,
    vecs,
    part_far,
    part_near,
    core_in,
    big_in,
    mid,
    small_in,
    last,
    z_in,
    fresh,
    dots_c,
    dots_x,
    dots_y,
    dots_z,
    load_sem,
    init_s,
    init_r,
    init_cs,
    init_cr,
    core_s,
    core_r,
    big_s,
    big_r,
    small_s,
    small_r,
    z_s,
    z_r,
    zg_s,
    zg_r,
    sg_s,
    sg_r,
    bg_s,
    bg_r,
    cg_s,
    cg_r,
    dot_s,
    dot_r,
):
    t = lax.axis_index("term")
    y = lax.axis_index("sector")
    z = t // 8
    x = lax.rem(t // 2, 4)
    c = lax.rem(t, 2)
    d = 1 - c

    def device(z_, x_, c_, y_):
        return ((z_ * 4 + x_) * 2 + c_, y_)

    def x_to(k):
        return device(z, lax.rem(x + k, 4), c, y)

    def y_to(k):
        return device(z, x, c, lax.rem(y + k, 4))

    def z_to(k):
        return device(lax.rem(z + k, 8), x, c, y)

    sibling = device(z, x, d, y)

    loads = []
    for index, (source, target) in enumerate(((right_hbm, right), (left_hbm, left))):
        load = pltpu.make_async_copy(source, target, load_sem.at[index])
        load.start()
        loads.append(load)

    barrier = pltpu.get_barrier_semaphore()
    peers = [sibling]
    peers += [x_to(k) for k in (1, 2, 3)]
    peers += [y_to(k) for k in (1, 2, 3)]
    peers += [z_to(k) for k in range(1, 8)]
    for peer in peers:
        pl.semaphore_signal(barrier, inc=1, device_id=peer, device_id_type=pl.DeviceIdType.MESH)

    sent = []

    def send(source, target, send_sem, recv_sem, peer):
        copy = pltpu.make_async_remote_copy(
            src_ref=source,
            dst_ref=target,
            send_sem=send_sem,
            recv_sem=recv_sem,
            device_id=peer,
            device_id_type=pl.DeviceIdType.MESH,
        )
        copy.start()
        sent.append(copy)
        return copy

    first = vecs.at[0]
    for cc in range(2):
        for xx in range(4):
            row = 96 * xx + 48 * cc
            first[cc, 0, xx, y] = psi[0, row : row + 24].reshape(3, 8, N)
            first[cc, 1, y, xx] = psi[0, row + 24 : row + 48].reshape(3, 8, N)

    pl.semaphore_wait(barrier, len(peers))

    near = []
    whole = []
    for k in (1, 2, 3):
        here = first.at[c, 0, x, y]
        near.append(send(here, here, init_s.at[0, k - 1], init_r.at[0, k - 1], y_to(k)))
    for k in (1, 2, 3):
        here = first.at[c, 1, y]
        whole.append(send(here, here, init_s.at[1, k - 1], init_r.at[1, k - 1], y_to(k)))

    loads[0].wait()

    def split_right(j, carry):
        high, low = halves(right[j].T)
        right3[j, 0:N] = high
        right3[j, N : 2 * N] = high
        right3[j, 2 * N :] = low
        return carry

    lax.fori_loop(0, 4, split_right, 0)

    forward = {}
    crossing = []
    for k in (1, 2, 3):
        near[k - 1].wait_recv()
        from_y = lax.rem(y + 4 - k, 4)
        here = first.at[c, 0, x, from_y]
        for m in (1, 2, 3):
            forward[k, m] = send(
                here, here, init_s.at[1 + k, m - 1], init_r.at[1 + k, m - 1], x_to(m)
            )
        crossing.append(send(here, here, init_cs.at[k - 1, 0], init_cr.at[k - 1, 0], sibling))

    loads[1].wait()

    def split_left(j, carry):
        for cc in range(2):
            for xx in range(4):
                row = 96 * xx + 48 * cc
                high, low = halves(left[j, row : row + 48])
                rows = slice(48 * xx, 48 * xx + 48)
                left3[j, cc, rows, 0:N] = high
                left3[j, cc, rows, N : 2 * N] = high
                left3[j, cc, rows, 2 * N :] = low
        return carry

    lax.fori_loop(0, 4, split_left, 0)

    for k in (1, 2, 3):
        whole[k - 1].wait_recv()
        here = first.at[c, 1, lax.rem(y + 4 - k, 4)]
        crossing.append(send(here, here, init_cs.at[k - 1, 4], init_cr.at[k - 1, 4], sibling))
    for k in (1, 2, 3):
        for m in (1, 2, 3):
            forward[k, m].wait_recv()
            here = first.at[c, 0, lax.rem(x + 4 - m, 4), lax.rem(y + 4 - k, 4)]
            crossing.append(send(here, here, init_cs.at[k - 1, m], init_cr.at[k - 1, m], sibling))
    for copy in crossing:
        copy.wait_recv()

    row0 = pl.multiple_of(96 * x + 48 * c + 8 * z, 8)
    for step in range(STEPS):
        vec = vecs.at[step]

        def convert(index, total):
            yy, xx = index // 4, lax.rem(index, 4)
            for cc in range(2):
                top = vec[cc, 0, xx, yy].reshape(24, N)
                low_rows = vec[cc, 1, yy, xx].reshape(24, N)
                block = jnp.concatenate([top, low_rows], axis=0)
                total = total + jnp.sum((block * block).reshape(6, 8, N), axis=0)
                high, low = halves(block)
                rows = pl.ds(pl.multiple_of(96 * xx + 48 * cc, 16), 48)
                vec3[yy, rows, 0:N] = high
                vec3[yy, rows, N : 2 * N] = low
                vec3[yy, rows, 2 * N :] = high
            return total

        squares = lax.fori_loop(0, 16, convert, jnp.zeros((8, N), F32))
        mean_square = jnp.sum(squares, axis=(0, 1), keepdims=True) / CELLS + EPSILON
        inverse = 1.0 / jnp.sqrt(mean_square)

        for j in range(4):
            high, low = halves(matmul(vec3[pair_in[0, j]], right3[j]))
            inner3[j, 0:N] = high
            inner3[j, N : 2 * N] = low
            inner3[j, 2 * N :] = high

        count = pair_count[0]
        chosen = [
            [jnp.logical_and(pair_out[0, j] == yy, count > j) for yy in range(4)] for j in range(4)
        ]

        def products(side, target):
            for j in range(4):
                product[j] = matmul(left3[j, side], inner3[j])

            def combine(xx, total):
                for cls in range(2):
                    rows = pl.ds(pl.multiple_of(48 * xx + 24 * cls, 8), 24)
                    blocks = [product[j, rows].reshape(3, 8, N) for j in range(4)]
                    for yy in range(4):
                        p, q = (xx, yy) if cls == 0 else (yy, xx)
                        value = jnp.where(chosen[0][yy], blocks[0], 0.0)
                        for j in range(1, 4):
                            value = value + jnp.where(chosen[j][yy], blocks[j], 0.0)
                        target[cls, p, q] = value
                        total = total + jnp.sum(value * vec[side, cls, p, q], axis=0)
                return total

            return lax.fori_loop(0, 4, combine, jnp.zeros((8, N), F32))

        far, own = part_far.at[step], part_near.at[step]
        dot = products(d, far)
        core = send(far, core_in.at[step], core_s.at[step], core_r.at[step], sibling)
        dot = dot + products(c, own)
        dots_c[step, c] = dot[:, 0:128] + dot[:, 128:256] + dot[:, 256:384]
        here = dots_c.at[step, c]
        dot_copies = [send(here, here, dot_s.at[step, 0], dot_r.at[step, 0], sibling)]

        core.wait_recv()
        big = []
        for k in (1, 2, 3, 0):
            for cls in range(2):
                p = lax.rem((x if cls == 0 else y) + k, 4)
                own[cls, p] = own[cls, p] + core_in[step, cls, p]
                if k:
                    big.append(
                        send(
                            own.at[cls, p],
                            big_in.at[step, cls, k - 1],
                            big_s.at[step, cls, k - 1],
                            big_r.at[step, cls, k - 1],
                            (x_to if cls == 0 else y_to)(k),
                        )
                    )
        dot_copies[0].wait_recv()
        dots_x[step, x] = dots_c[step, 0] + dots_c[step, 1]
        here = dots_x.at[step, x]
        dot_copies = [
            send(here, here, dot_s.at[step, k], dot_r.at[step, k], x_to(k)) for k in (1, 2, 3)
        ]

        for copy in big:
            copy.wait_recv()
        small = []
        for k in (1, 2, 3, 0):
            for cls in range(2):
                p, q = (x, y) if cls == 0 else (y, x)
                q = lax.rem(q + k, 4)
                value = own[cls, p, q] + big_in[step, cls, 0, q]
                value = value + (big_in[step, cls, 1, q] + big_in[step, cls, 2, q])
                mid[step, cls, q] = value
                if k:
                    small.append(
                        send(
                            mid.at[step, cls, q],
                            small_in.at[step, cls, k - 1],
                            small_s.at[step, cls, k - 1],
                            small_r.at[step, cls, k - 1],
                            (y_to if cls == 0 else x_to)(k),
                        )
                    )
        for copy in dot_copies:
            copy.wait_recv()
        dots_y[step, y] = (dots_x[step, 0] + dots_x[step, 1]) + (dots_x[step, 2] + dots_x[step, 3])
        here = dots_y.at[step, y]
        dot_copies = [
            send(here, here, dot_s.at[step, 3 + k], dot_r.at[step, 3 + k], y_to(k))
            for k in (1, 2, 3)
        ]

        for copy in small:
            copy.wait_recv()
        for cls in range(2):
            q = y if cls == 0 else x
            value = mid[step, cls, q] + small_in[step, cls, 0]
            last[step, cls] = value + (small_in[step, cls, 1] + small_in[step, cls, 2])

        def z_copy(k):
            to = lax.rem(z + k, 8)
            return pltpu.make_async_remote_copy(
                src_ref=last.at[step, to // 3, lax.rem(to, 3)],
                dst_ref=z_in.at[step, k - 1],
                send_sem=z_s.at[step, k - 1],
                recv_sem=z_r.at[step, k - 1],
                device_id=z_to(k),
                device_id_type=pl.DeviceIdType.MESH,
            )

        for k in range(1, 8):

            @pl.when(lax.rem(z + k, 8) < 6)
            def _():
                z_copy(k).start()

        for copy in dot_copies:
            copy.wait_recv()
        dots_z[step, z] = (dots_y[step, 0] + dots_y[step, 1]) + (dots_y[step, 2] + dots_y[step, 3])
        here = dots_z.at[step, z]
        dot_copies = [
            send(here, here, dot_s.at[step, 6 + k], dot_r.at[step, 6 + k], z_to(k))
            for k in range(1, 8)
        ]
        for copy in dot_copies:
            copy.wait_recv()
        pairs = [dots_z[step, 2 * i] + dots_z[step, 2 * i + 1] for i in range(4)]
        tile = (pairs[0] + pairs[1]) + (pairs[2] + pairs[3])
        rayleigh = jnp.sum(tile, axis=(0, 1), keepdims=True) * (inverse * inverse) / CELLS
        energies[step] = jnp.sum(rayleigh)

        final = step == STEPS - 1

        def zg_copy(k):
            if final:
                here = out.at[0, pl.ds(row0, 8)]
            else:
                here = fresh.at[z // 3, lax.rem(z, 3)]
            return pltpu.make_async_remote_copy(
                src_ref=here,
                dst_ref=here,
                send_sem=zg_s.at[step, k - 1],
                recv_sem=zg_r.at[step, k - 1],
                device_id=z_to(k),
                device_id_type=pl.DeviceIdType.MESH,
            )

        def zg_wait(k):
            return pltpu.make_async_remote_copy(
                src_ref=z_in.at[step, 0],
                dst_ref=z_in.at[step, 0],
                send_sem=zg_s.at[step, k - 1],
                recv_sem=zg_r.at[step, k - 1],
                device_id=z_to(k),
                device_id_type=pl.DeviceIdType.MESH,
            )

        @pl.when(z < 6)
        def _():
            for k in range(1, 8):
                pltpu.make_async_remote_copy(
                    src_ref=z_in.at[step, k - 1],
                    dst_ref=z_in.at[step, k - 1],
                    send_sem=z_s.at[step, k - 1],
                    recv_sem=z_r.at[step, k - 1],
                    device_id=z_to(k),
                    device_id_type=pl.DeviceIdType.MESH,
                ).wait_recv()
            total = last[step, z // 3, lax.rem(z, 3)]
            for k in range(7):
                total = total + z_in[step, k]
            if step == 0:
                old = psi[0, pl.ds(row0, 8)]
            else:
                old = fresh[z // 3, lax.rem(z, 3)]
            normed = old * inverse
            residual = total * inverse - rayleigh * normed
            scale = jnp.maximum(jnp.abs(diagonal[0, pl.ds(row0, 8)] - rayleigh), 1.0)
            new = normed - residual / scale
            if final:
                out[0, pl.ds(row0, 8)] = new
            else:
                fresh[z // 3, lax.rem(z, 3)] = new
            for k in range(1, 8):
                zg_copy(k).start()

        for k in range(1, 8):

            @pl.when(lax.rem(z + 8 - k, 8) < 6)
            def _():
                zg_wait(k).wait_recv()

        if not final:
            after = vecs.at[step + 1]
            grown = []
            for cls in range(2):
                p, q = (x, y) if cls == 0 else (y, x)
                after[c, cls, p, q] = fresh[cls]
                for k in (1, 2, 3):
                    grown.append(
                        send(
                            fresh.at[cls],
                            after.at[c, cls, p, q],
                            sg_s.at[cls, k - 1],
                            sg_r.at[cls, k - 1],
                            (y_to if cls == 0 else x_to)(k),
                        )
                    )
            for copy in grown:
                copy.wait_recv()
            wide = {}
            crossing = []
            for k in (1, 2, 3):
                for cls in range(2):
                    here = after.at[c, cls, x if cls == 0 else y]
                    wide[cls, k] = send(
                        here,
                        here,
                        bg_s.at[cls, k - 1],
                        bg_r.at[cls, k - 1],
                        (x_to if cls == 0 else y_to)(k),
                    )
            for k in (0, 1, 2, 3):
                for cls in range(2):
                    if k:
                        wide[cls, k].wait_recv()
                    here = after.at[c, cls, lax.rem((x if cls == 0 else y) + 4 - k, 4)]
                    crossing.append(
                        send(here, here, cg_s.at[cls, k], cg_r.at[cls, k], sibling)
                    )
            for copy in crossing:
                copy.wait_recv()
        else:
            rows = pl.ds(pl.multiple_of(96 * x + 48 * c, 8), 48)
            here = out.at[0, rows]
            wide = [None]
            crossing = []
            for k in (1, 2, 3):
                wide.append(send(here, here, bg_s.at[2, k - 1], bg_r.at[2, k - 1], x_to(k)))
            for k in (0, 1, 2, 3):
                if k:
                    wide[k].wait_recv()
                rows = pl.ds(pl.multiple_of(96 * lax.rem(x + 4 - k, 4) + 48 * c, 8), 48)
                here = out.at[0, rows]
                crossing.append(send(here, here, cg_s.at[2, k], cg_r.at[2, k], sibling))
            for copy in crossing:
                copy.wait_recv()

        for k in range(1, 8):

            @pl.when(lax.rem(z + k, 8) < 6)
            def _():
                z_copy(k).wait_send()

        @pl.when(z < 6)
        def _():
            for k in range(1, 8):
                zg_copy(k).wait_send()

    for copy in sent:
        copy.wait_send()


def shards(psi_start, diagonal, left_ops, right_ops, pair_in, pair_out, pair_count):
    vmem = pl.BlockSpec(memory_space=pltpu.VMEM)
    smem = pl.BlockSpec(memory_space=pltpu.SMEM)
    hbm = pl.BlockSpec(memory_space=pl.ANY)
    dma = pltpu.SemaphoreType.DMA
    rows = (3, 8, N)
    return pl.pallas_call(
        kernel,
        out_shape=(
            jax.ShapeDtypeStruct((1, N, N), F32),
            jax.ShapeDtypeStruct((STEPS,), F32),
        ),
        in_specs=[smem, smem, smem, vmem, vmem, hbm, hbm],
        out_specs=(vmem, smem),
        scratch_shapes=[
            pltpu.VMEM((4, N, N), F32),
            pltpu.VMEM((4, N, N), F32),
            pltpu.VMEM((4, 2, N // 2, 3 * N), BF16),
            pltpu.VMEM((4, 3 * N, N), BF16),
            pltpu.VMEM((4, N, 3 * N), BF16),
            pltpu.VMEM((4, 3 * N, N), BF16),
            pltpu.VMEM((4, N // 2, N), F32),
            pltpu.VMEM((STEPS, 2, 2, 4, 4, *rows), F32),
            pltpu.VMEM((STEPS, 2, 4, 4, *rows), F32),
            pltpu.VMEM((STEPS, 2, 4, 4, *rows), F32),
            pltpu.VMEM((STEPS, 2, 4, 4, *rows), F32),
            pltpu.VMEM((STEPS, 2, 3, 4, *rows), F32),
            pltpu.VMEM((STEPS, 2, 4, *rows), F32),
            pltpu.VMEM((STEPS, 2, 3, *rows), F32),
            pltpu.VMEM((STEPS, 2, *rows), F32),
            pltpu.VMEM((STEPS, 7, 8, N), F32),
            pltpu.VMEM((2, *rows), F32),
            pltpu.VMEM((STEPS, 2, 8, 128), F32),
            pltpu.VMEM((STEPS, 4, 8, 128), F32),
            pltpu.VMEM((STEPS, 4, 8, 128), F32),
            pltpu.VMEM((STEPS, 8, 8, 128), F32),
            dma((2,)),
            dma((5, 3)),
            dma((5, 3)),
            dma((3, 5)),
            dma((3, 5)),
            dma((STEPS,)),
            dma((STEPS,)),
            dma((STEPS, 2, 3)),
            dma((STEPS, 2, 3)),
            dma((STEPS, 2, 3)),
            dma((STEPS, 2, 3)),
            dma((STEPS, 7)),
            dma((STEPS, 7)),
            dma((STEPS, 7)),
            dma((STEPS, 7)),
            dma((2, 3)),
            dma((2, 3)),
            dma((3, 3)),
            dma((3, 3)),
            dma((3, 4)),
            dma((3, 4)),
            dma((STEPS, 14)),
            dma((STEPS, 14)),
        ],
        compiler_params=pltpu.CompilerParams(
            collective_id=0, has_side_effects=True, vmem_limit_bytes=52 * 1024 * 1024
        ),
    )(pair_in, pair_out, pair_count, psi_start, diagonal, left_ops, right_ops)


def solution(mesh):
    both = ("term", "sector")
    in_specs = (
        P("sector", None, None),
        P("sector", None, None),
        P(both, None, None),
        P(both, None, None),
        P(both, None),
        P(both, None),
        P(both),
    )
    out_specs = (P("sector", None, None), P())
    return jax.shard_map(
        shards, mesh=mesh, in_specs=in_specs, out_specs=out_specs, check_vma=False
    )
```

```python
import functools

import jax
import jax.numpy as jnp
from jax import lax
from jax.experimental import pallas as pl
from jax.experimental.pallas import tpu as pltpu
from jax.sharding import PartitionSpec as P

STEPS = 2
EPSILON = 1e-06
N = 384
CELLS = float(4 * N * N)
F32 = jnp.float32
BF16 = jnp.bfloat16


def matmul(a, b):
    return lax.dot_general(a, b, (((1,), (0,)), ((), ())), preferred_element_type=F32)


def halves(value):
    high = value.astype(BF16)
    return high, (value - high.astype(F32)).astype(BF16)


def kernel(
    pair_in_hbm,
    pair_out_hbm,
    pair_count_hbm,
    psi_hbm,
    diagonal_hbm,
    left_hbm,
    right_hbm,
    out,
    energies,
    pair_in,
    pair_out,
    pair_count,
    psi,
    diagonal,
    left,
    right,
    left3,
    right3,
    vec3,
    inner3,
    product,
    vecs,
    part_far,
    part_near,
    core_in,
    big_in,
    mid,
    small_in,
    last,
    z_in,
    fresh,
    dots_c,
    dots_z,
    dots_x,
    dots_y,
    load_sem,
    init_s,
    init_r,
    init_cs,
    init_cr,
    core_s,
    core_r,
    big_s,
    big_r,
    small_s,
    small_r,
    z_s,
    z_r,
    zg_s,
    zg_r,
    sg_s,
    sg_r,
    bg_s,
    bg_r,
    cg_s,
    cg_r,
    dot_s,
    dot_r,
):
    t = lax.axis_index("term")
    y = lax.axis_index("sector")
    z = t // 8
    x = lax.rem(t // 2, 4)
    c = lax.rem(t, 2)
    d = 1 - c

    def device(z_, x_, c_, y_):
        return ((z_ * 4 + x_) * 2 + c_, y_)

    def x_to(k):
        return device(z, lax.rem(x + k, 4), c, y)

    def y_to(k):
        return device(z, x, c, lax.rem(y + k, 4))

    def z_to(k):
        return device(lax.rem(z + k, 8), x, c, y)

    sibling = device(z, x, d, y)

    p_me, q_me = (x, y), (y, x)
    p_to, q_to = (x_to, y_to), (y_to, x_to)

    barrier = pltpu.get_barrier_semaphore()
    peers = [z_to(k) for k in (4, 3, 5, 2, 6, 1, 7)]
    peers += [x_to(k) for k in (2, 1, 3)]
    peers += [y_to(k) for k in (2, 1, 3)]
    peers += [sibling]
    for peer in peers:
        pl.semaphore_signal(barrier, inc=1, device_id=peer, device_id_type=pl.DeviceIdType.MESH)

    loads = {}
    for index, (name, source, target) in enumerate(
        (
            ("psi", psi_hbm, psi),
            ("right", right_hbm, right),
            ("left", left_hbm, left),
            ("in", pair_in_hbm, pair_in),
            ("out", pair_out_hbm, pair_out),
            ("count", pair_count_hbm, pair_count),
            ("diagonal", diagonal_hbm, diagonal),
        )
    ):
        loads[name] = pltpu.make_async_copy(source, target, load_sem.at[index])
        loads[name].start()

    sent = []

    def remote(source, target, send_sem, recv_sem, peer):
        return pltpu.make_async_remote_copy(
            src_ref=source,
            dst_ref=target,
            send_sem=send_sem,
            recv_sem=recv_sem,
            device_id=peer,
            device_id_type=pl.DeviceIdType.MESH,
        )

    def send(source, target, send_sem, recv_sem, peer):
        copy = remote(source, target, send_sem, recv_sem, peer)
        copy.start()
        sent.append(copy)
        return copy

    first = vecs.at[0]
    loads["psi"].wait()
    for cc in range(2):
        for xx in range(4):
            row = 96 * xx + 48 * cc
            first[cc, 0, y, xx] = psi[0, row : row + 24].reshape(3, 8, N)
            first[cc, 1, xx, y] = psi[0, row + 24 : row + 48].reshape(3, 8, N)

    loads["right"].wait()

    def split_right(j, carry):
        high, low = halves(right[j].T)
        right3[j, 0:N] = high
        right3[j, N : 2 * N] = high
        right3[j, 2 * N :] = low
        return carry

    lax.fori_loop(0, 4, split_right, 0)

    pl.semaphore_wait(barrier, len(peers))

    near = []
    whole = []
    for k in (1, 2, 3):
        here = first.at[c, 0, y, x]
        near.append(send(here, here, init_s.at[0, k - 1], init_r.at[0, k - 1], y_to(k)))
    for k in (1, 2, 3):
        here = first.at[c, 1, :, y]
        whole.append(send(here, here, init_s.at[1, k - 1], init_r.at[1, k - 1], y_to(k)))

    loads["left"].wait()

    def split_left(j, carry):
        for cc in range(2):
            for xx in range(4):
                row = 96 * xx + 48 * cc
                high, low = halves(left[j, row : row + 48])
                rows = slice(48 * xx, 48 * xx + 48)
                left3[j, cc, rows, 0:N] = high
                left3[j, cc, rows, N : 2 * N] = high
                left3[j, cc, rows, 2 * N :] = low
        return carry

    lax.fori_loop(0, 4, split_left, 0)

    forward = {}
    crossing = []
    for k in (1, 3, 2):
        near[k - 1].wait_recv()
        here = first.at[c, 0, lax.rem(y + 4 - k, 4), x]
        for m in (1, 2, 3):
            forward[k, m] = send(
                here, here, init_s.at[1 + k, m - 1], init_r.at[1 + k, m - 1], x_to(m)
            )
        crossing.append(send(here, here, init_cs.at[k - 1, 0], init_cr.at[k - 1, 0], sibling))
    for name in ("in", "out", "count", "diagonal"):
        loads[name].wait()
    for k in (1, 3, 2):
        for m in (1, 3, 2):
            forward[k, m].wait_recv()
            here = first.at[c, 0, lax.rem(y + 4 - k, 4), lax.rem(x + 4 - m, 4)]
            crossing.append(send(here, here, init_cs.at[k - 1, m], init_cr.at[k - 1, m], sibling))
        whole[k - 1].wait_recv()
        here = first.at[c, 1, :, lax.rem(y + 4 - k, 4)]
        crossing.append(send(here, here, init_cs.at[k - 1, 4], init_cr.at[k - 1, 4], sibling))
    for copy in crossing:
        copy.wait_recv()

    for step in range(STEPS):
        finish_step = davidson_step(
            step, c, d, x, y, z, p_me, q_me, p_to, q_to, z_to, device, sibling, remote, send,
            out, energies, pair_in, pair_out, pair_count, psi, diagonal,
            left3, right3, vec3, inner3, product, vecs, part_far, part_near, core_in, big_in, mid,
            small_in, last, z_in, fresh, dots_c, dots_z, dots_x, dots_y,
            core_s, core_r, big_s, big_r, small_s, small_r, z_s, z_r, zg_s, zg_r,
            sg_s, sg_r, bg_s, bg_r, cg_s, cg_r, dot_s, dot_r,
        )
        finish_step()

    for copy in sent:
        copy.wait_send()


def davidson_step(
    step, c, d, x, y, z, p_me, q_me, p_to, q_to, z_to, device, sibling, remote, send,
    out, energies, pair_in, pair_out, pair_count, psi, diagonal,
    left3, right3, vec3, inner3, product, vecs, part_far, part_near, core_in, big_in, mid,
    small_in, last, z_in, fresh, dots_c, dots_z, dots_x, dots_y,
    core_s, core_r, big_s, big_r, small_s, small_r, z_s, z_r, zg_s, zg_r,
    sg_s, sg_r, bg_s, bg_r, cg_s, cg_r, dot_s, dot_r,
):
    final = step == STEPS - 1
    vec = vecs.at[step]
    row0 = pl.multiple_of(96 * x + 48 * c + 8 * z, 8)

    def convert(index, total):
        yy, xx = index // 4, lax.rem(index, 4)
        for cc in range(2):
            top = vec[cc, 0, yy, xx].reshape(24, N)
            bottom = vec[cc, 1, xx, yy].reshape(24, N)
            block = jnp.concatenate([top, bottom], axis=0)
            total = total + jnp.sum((block * block).reshape(6, 8, N), axis=0)
            high, low = halves(block)
            rows = pl.ds(pl.multiple_of(96 * xx + 48 * cc, 16), 48)
            vec3[yy, rows, 0:N] = high
            vec3[yy, rows, N : 2 * N] = low
            vec3[yy, rows, 2 * N :] = high
        return total

    squares = lax.fori_loop(0, 16, convert, jnp.zeros((8, N), F32))

    for j in range(4):
        high, low = halves(matmul(vec3[pair_in[0, j]], right3[j]))
        inner3[j, 0:N] = high
        inner3[j, N : 2 * N] = low
        inner3[j, 2 * N :] = high

    count = pair_count[0]
    targets = [pair_out[0, j] for j in range(4)]

    def combine(side, cls, q, store, total):
        def one(p, total):
            xx, yy = (p, q) if cls == 0 else (q, p)
            rows = pl.ds(pl.multiple_of(48 * xx + 24 * cls, 8), 24)
            value = jnp.zeros((24, N), F32)
            for j in range(4):
                live = jnp.logical_and(targets[j] == yy, count > j)
                value = value + jnp.where(live, product[j, rows], 0.0)
            value = value.reshape(3, 8, N)
            store(p, value)
            return total + jnp.sum(value * vec[side, cls, q, p], axis=0)

        return lax.fori_loop(0, 4, one, total)

    far, own = part_far.at[step], part_near.at[step]
    dot = jnp.zeros((8, N), F32)
    for j in range(4):
        product[j] = matmul(left3[j, d], inner3[j])
    core = {}
    for k in (1, 2, 3, 0):
        for cls in range(2):
            q = lax.rem(q_me[cls] + k, 4)

            def store_far(p, value, cls=cls, q=q):
                far[cls, q, p] = value

            dot = combine(d, cls, q, store_far, dot)
            core[cls, k] = send(
                far.at[cls, q],
                core_in.at[step, cls, q],
                core_s.at[step, cls, k],
                core_r.at[step, cls, k],
                sibling,
            )
    for j in range(4):
        product[j] = matmul(left3[j, c], inner3[j])
    big = {}
    for k in (1, 2, 3, 0):
        for cls in range(2):
            q = lax.rem(q_me[cls] + k, 4)
            core[cls, k].wait_recv()

            def store_near(p, value, cls=cls, q=q):
                own[cls, q, p] = value + core_in[step, cls, q, p]

            dot = combine(c, cls, q, store_near, dot)
            for m in (2, 1, 3):
                big[cls, k, m] = send(
                    own.at[cls, q, lax.rem(p_me[cls] + m, 4)],
                    big_in.at[step, cls, k, m - 1],
                    big_s.at[step, cls, k, m - 1],
                    big_r.at[step, cls, k, m - 1],
                    p_to[cls](m),
                )

    dots_c[step, c] = dot[:, 0:128] + dot[:, 128:256] + dot[:, 256:384]
    here = dots_c.at[step, c]
    send(here, here, dot_s.at[step, 0], dot_r.at[step, 0], sibling).wait_recv()
    dots_z[step, z] = dots_c[step, 0] + dots_c[step, 1]
    here = dots_z.at[step, z]
    dots = [send(here, here, dot_s.at[step, k], dot_r.at[step, k], z_to(k)) for k in range(1, 8)]

    mean_square = jnp.sum(squares, axis=(0, 1), keepdims=True) / CELLS + EPSILON
    inverse = 1.0 / jnp.sqrt(mean_square)

    small = {}
    for k in (1, 2, 3, 0):
        for cls in range(2):
            for m in (1, 2, 3):
                big[cls, k, m].wait_recv()
            q = lax.rem(q_me[cls] + k, 4)
            value = own[cls, q, p_me[cls]] + big_in[step, cls, k, 0]
            value = value + (big_in[step, cls, k, 1] + big_in[step, cls, k, 2])
            mid[step, cls, q] = value
            if k:
                small[cls, k] = send(
                    mid.at[step, cls, q],
                    small_in.at[step, cls, k - 1],
                    small_s.at[step, cls, k - 1],
                    small_r.at[step, cls, k - 1],
                    q_to[cls](k),
                )
        if k == 2:
            for copy in dots:
                copy.wait_recv()
            pairs = [dots_z[step, 2 * i] + dots_z[step, 2 * i + 1] for i in range(4)]
            dots_x[step, x] = (pairs[0] + pairs[1]) + (pairs[2] + pairs[3])
            here = dots_x.at[step, x]
            dots = [
                send(here, here, dot_s.at[step, 7 + m], dot_r.at[step, 7 + m], p_to[0](m))
                for m in (1, 2, 3)
            ]
    for copy in dots:
        copy.wait_recv()
    dots_y[step, y] = (dots_x[step, 0] + dots_x[step, 1]) + (dots_x[step, 2] + dots_x[step, 3])
    here = dots_y.at[step, y]
    dots = [
        send(here, here, dot_s.at[step, 10 + m], dot_r.at[step, 10 + m], p_to[1](m))
        for m in (1, 2, 3)
    ]

    def to_owner(owner):
        slot = lax.rem(owner - z + 8, 8) - 1
        return remote(
            last.at[step, owner // 3, owner % 3],
            z_in.at[step, slot],
            z_s.at[step, owner],
            z_r.at[step, slot],
            device(owner, x, c, y),
        )

    for cls in range(2):
        for k in (1, 2, 3):
            small[cls, k].wait_recv()
        value = mid[step, cls, q_me[cls]] + small_in[step, cls, 0]
        last[step, cls] = value + (small_in[step, cls, 1] + small_in[step, cls, 2])
        for owner in range(3 * cls, 3 * cls + 3):

            @pl.when(z != owner)
            def _(owner=owner):
                to_owner(owner).start()

    for copy in dots:
        copy.wait_recv()
    tile = (dots_y[step, 0] + dots_y[step, 1]) + (dots_y[step, 2] + dots_y[step, 3])
    rayleigh = jnp.sum(tile, axis=(0, 1), keepdims=True) * (inverse * inverse) / CELLS

    def from_owner(owner, peer):
        if final:
            here = out.at[0, pl.ds(pl.multiple_of(96 * x + 48 * c + 8 * owner, 8), 8)]
        else:
            here = fresh.at[owner // 3, lax.rem(owner, 3)]
        return here, peer

    def spread(k):
        here, peer = from_owner(z, z_to(k))
        return remote(here, here, zg_s.at[step, k - 1], zg_r.at[step, z], peer)

    @pl.when(z < 6)
    def _():
        if step == 0:
            old = psi[0, pl.ds(row0, 8)]
        else:
            old = fresh[z // 3, lax.rem(z, 3)]
        normed = old * inverse
        scale = jnp.maximum(jnp.abs(diagonal[0, pl.ds(row0, 8)] - rayleigh), 1.0)
        total = last[step, z // 3, lax.rem(z, 3)]
        for k in range(1, 8):
            remote(
                z_in.at[step, k - 1],
                z_in.at[step, k - 1],
                z_s.at[step, 0],
                z_r.at[step, k - 1],
                z_to(k),
            ).wait_recv()
            total = total + z_in[step, k - 1]
        residual = total * inverse - rayleigh * normed
        new = normed - residual / scale
        if final:
            out[0, pl.ds(row0, 8)] = new
        else:
            fresh[z // 3, lax.rem(z, 3)] = new
        for k in (4, 3, 5, 2, 6, 1, 7):
            spread(k).start()

    energies[step] = jnp.sum(rayleigh)

    def wait_owners(cls):
        for owner in range(3 * cls, 3 * cls + 3):

            @pl.when(z != owner)
            def _(owner=owner):
                remote(
                    z_in.at[step, 0],
                    z_in.at[step, 0],
                    zg_s.at[step, 0],
                    zg_r.at[step, owner],
                    device(owner, x, c, y),
                ).wait_recv()

    wide = {}
    crossing = []
    if not final:
        after = vecs.at[step + 1]
        grown = {}
        for cls in range(2):
            wait_owners(cls)
            here, there = fresh.at[cls], after.at[c, cls, q_me[cls], p_me[cls]]
            for k in (2, 1, 3):
                grown[cls, k] = send(
                    here, there, sg_s.at[cls, k - 1], sg_r.at[cls, k - 1], q_to[cls](k)
                )
            for m in (2, 1, 3):
                wide[cls, 0, m] = send(
                    here, there, bg_s.at[cls, 0, m - 1], bg_r.at[cls, 0, m - 1], p_to[cls](m)
                )
            crossing.append(send(here, there, cg_s.at[cls, 0, 0], cg_r.at[cls, 0, 0], sibling))
            after[c, cls, q_me[cls], p_me[cls]] = fresh[cls]
        for k in (1, 3, 2):
            for cls in range(2):
                grown[cls, k].wait_recv()
                here = after.at[c, cls, lax.rem(q_me[cls] + 4 - k, 4), p_me[cls]]
                for m in (2, 1, 3):
                    wide[cls, k, m] = send(
                        here, here, bg_s.at[cls, k, m - 1], bg_r.at[cls, k, m - 1], p_to[cls](m)
                    )
                crossing.append(send(here, here, cg_s.at[cls, k, 0], cg_r.at[cls, k, 0], sibling))
        for k in (0, 1, 3, 2):
            for m in (1, 3, 2):
                for cls in range(2):
                    wide[cls, k, m].wait_recv()
                    q, p = lax.rem(q_me[cls] + 4 - k, 4), lax.rem(p_me[cls] + 4 - m, 4)
                    here = after.at[c, cls, q, p]
                    crossing.append(
                        send(here, here, cg_s.at[cls, k, m], cg_r.at[cls, k, m], sibling)
                    )
    else:

        def rows(cls, xx):
            return out.at[0, pl.ds(pl.multiple_of(96 * xx + 48 * c + 24 * cls, 8), 24)]

        for cls in range(2):
            wait_owners(cls)
            here = rows(cls, x)
            for m in (2, 1, 3):
                wide[cls, m] = send(
                    here, here, bg_s.at[cls, 4, m - 1], bg_r.at[cls, 4, m - 1], p_to[0](m)
                )
            crossing.append(send(here, here, cg_s.at[cls, 4, 0], cg_r.at[cls, 4, 0], sibling))
        for m in (1, 3, 2):
            for cls in range(2):
                wide[cls, m].wait_recv()
                here = rows(cls, lax.rem(x + 4 - m, 4))
                crossing.append(send(here, here, cg_s.at[cls, 4, m], cg_r.at[cls, 4, m], sibling))
    for copy in crossing:
        copy.wait_recv()

    def finish():
        for owner in range(6):

            @pl.when(z != owner)
            def _(owner=owner):
                to_owner(owner).wait_send()

        @pl.when(z < 6)
        def _():
            for k in range(1, 8):
                spread(k).wait_send()

    return finish


def shards(psi_start, diagonal, left_ops, right_ops, pair_in, pair_out, pair_count):
    vmem = pl.BlockSpec(memory_space=pltpu.VMEM)
    smem = pl.BlockSpec(memory_space=pltpu.SMEM)
    hbm = pl.BlockSpec(memory_space=pl.ANY)
    dma = pltpu.SemaphoreType.DMA
    rows = (3, 8, N)
    pieces = (2, 4, 4, *rows)
    return pl.pallas_call(
        kernel,
        out_shape=(
            jax.ShapeDtypeStruct((1, N, N), F32),
            jax.ShapeDtypeStruct((STEPS,), F32),
        ),
        in_specs=[hbm] * 7,
        out_specs=(vmem, smem),
        scratch_shapes=[
            pltpu.SMEM((1, 4), jnp.int32),
            pltpu.SMEM((1, 4), jnp.int32),
            pltpu.SMEM((1,), jnp.int32),
            pltpu.VMEM((1, N, N), F32),
            pltpu.VMEM((1, N, N), F32),
            pltpu.VMEM((4, N, N), F32),
            pltpu.VMEM((4, N, N), F32),
            pltpu.VMEM((4, 2, N // 2, 3 * N), BF16),
            pltpu.VMEM((4, 3 * N, N), BF16),
            pltpu.VMEM((4, N, 3 * N), BF16),
            pltpu.VMEM((4, 3 * N, N), BF16),
            pltpu.VMEM((4, N // 2, N), F32),
            pltpu.VMEM((STEPS, 2, *pieces), F32),
            pltpu.VMEM((STEPS, *pieces), F32),
            pltpu.VMEM((STEPS, *pieces), F32),
            pltpu.VMEM((STEPS, *pieces), F32),
            pltpu.VMEM((STEPS, 2, 4, 3, *rows), F32),
            pltpu.VMEM((STEPS, 2, 4, *rows), F32),
            pltpu.VMEM((STEPS, 2, 3, *rows), F32),
            pltpu.VMEM((STEPS, 2, *rows), F32),
            pltpu.VMEM((STEPS, 7, 8, N), F32),
            pltpu.VMEM((2, *rows), F32),
            pltpu.VMEM((STEPS, 2, 8, 128), F32),
            pltpu.VMEM((STEPS, 8, 8, 128), F32),
            pltpu.VMEM((STEPS, 4, 8, 128), F32),
            pltpu.VMEM((STEPS, 4, 8, 128), F32),
            dma((7,)),
            dma((5, 3)),
            dma((5, 3)),
            dma((3, 5)),
            dma((3, 5)),
            dma((STEPS, 2, 4)),
            dma((STEPS, 2, 4)),
            dma((STEPS, 2, 4, 3)),
            dma((STEPS, 2, 4, 3)),
            dma((STEPS, 2, 3)),
            dma((STEPS, 2, 3)),
            dma((STEPS, 6)),
            dma((STEPS, 7)),
            dma((STEPS, 7)),
            dma((STEPS, 6)),
            dma((2, 3)),
            dma((2, 3)),
            dma((2, 5, 3)),
            dma((2, 5, 3)),
            dma((2, 5, 4)),
            dma((2, 5, 4)),
            dma((STEPS, 14)),
            dma((STEPS, 14)),
        ],
        compiler_params=pltpu.CompilerParams(
            collective_id=0, has_side_effects=True, vmem_limit_bytes=52 * 1024 * 1024
        ),
    )(pair_in, pair_out, pair_count, psi_start, diagonal, left_ops, right_ops)


def solution(mesh):
    both = ("term", "sector")
    in_specs = (
        P("sector", None, None),
        P("sector", None, None),
        P(both, None, None),
        P(both, None, None),
        P(both, None),
        P(both, None),
        P(both),
    )
    out_specs = (P("sector", None, None), P())
    return jax.shard_map(
        shards, mesh=mesh, in_specs=in_specs, out_specs=out_specs, check_vma=False
    )
```

```python
import functools

import jax
import jax.numpy as jnp
from jax import lax
from jax.experimental import pallas as pl
from jax.experimental.pallas import tpu as pltpu
from jax.sharding import PartitionSpec as P

STEPS = 2
EPSILON = 1e-06
N = 384
CELLS = float(4 * N * N)
F32 = jnp.float32
BF16 = jnp.bfloat16


def matmul(a, b):
    return lax.dot_general(a, b, (((1,), (0,)), ((), ())), preferred_element_type=F32)


def halves(value):
    high = value.astype(BF16)
    return high, (value - high.astype(F32)).astype(BF16)


def kernel(
    pair_in_hbm,
    pair_out_hbm,
    pair_count_hbm,
    psi,
    diagonal,
    left_hbm,
    right_hbm,
    out,
    energies,
    pair_in,
    pair_out,
    pair_count,
    diagonal_own,
    left,
    right,
    left3,
    right3,
    vec3,
    inner3,
    product,
    vecs,
    part_far,
    part_near,
    core_in,
    big_in,
    mid,
    small_in,
    last,
    z_in,
    fresh,
    dots,
    load_sem,
    near_s,
    near_r,
    whole_s,
    whole_r,
    forward_s,
    forward_r,
    core_s,
    core_r,
    big_s,
    big_r,
    small_s,
    small_r,
    z_s,
    z_r,
    owner_s,
    owner_r,
    grow_s,
    grow_r,
    wide_s,
    wide_r,
    cross_s,
    cross_r,
    end_s,
    end_r,
    dot_s,
    dot_r,
):
    t = lax.axis_index("term")
    y = lax.axis_index("sector")
    z = t // 8
    x = lax.rem(t // 2, 4)
    c = lax.rem(t, 2)
    d = 1 - c

    def device(z_, x_, c_, y_):
        return ((z_ * 4 + x_) * 2 + c_, y_)

    def x_to(k):
        return device(z, lax.rem(x + k, 4), c, y)

    def y_to(k):
        return device(z, x, c, lax.rem(y + k, 4))

    def z_to(k):
        return device(lax.rem(z + k, 8), x, c, y)

    sibling = device(z, x, d, y)

    p_me, q_me = (x, y), (y, x)
    p_to, q_to = (x_to, y_to), (y_to, x_to)

    barrier = pltpu.get_barrier_semaphore()
    peers = [z_to(k) for k in (4, 3, 5, 2, 6, 1, 7)]
    peers += [x_to(k) for k in (2, 1, 3)]
    peers += [y_to(k) for k in (2, 1, 3)]
    peers += [sibling]
    for peer in peers:
        pl.semaphore_signal(barrier, inc=1, device_id=peer, device_id_type=pl.DeviceIdType.MESH)

    first = vecs.at[0]
    owner = jnp.minimum(z, 5)
    loads = []
    for source, target in (
        (right_hbm, right),
        (left_hbm, left),
        (psi.at[x, c, owner // 3, lax.rem(owner, 3)], fresh.at[0, owner // 3, lax.rem(owner, 3)]),
        (diagonal.at[x, c, owner // 3, lax.rem(owner, 3)], diagonal_own),
        (psi.at[:, 0, 0], first.at[0, 0, y]),
        (psi.at[:, 1, 0], first.at[1, 0, y]),
        (psi.at[:, 0, 1], first.at[0, 1, :, y]),
        (psi.at[:, 1, 1], first.at[1, 1, :, y]),
        (pair_in_hbm, pair_in),
        (pair_out_hbm, pair_out),
        (pair_count_hbm, pair_count),
    ):
        load = pltpu.make_async_copy(source, target, load_sem.at[len(loads)])
        load.start()
        loads.append(load)

    def remote(source, target, send_sem, recv_sem, peer):
        return pltpu.make_async_remote_copy(
            src_ref=source,
            dst_ref=target,
            send_sem=send_sem,
            recv_sem=recv_sem,
            device_id=peer,
            device_id_type=pl.DeviceIdType.MESH,
        )

    def send(source, target, send_sem, recv_sem, peer):
        remote(source, target, send_sem, recv_sem, peer).start()

    def arrived(like, sem):
        remote(like, like, sem, sem, sibling).wait_recv()

    def left_here(like, sem):
        remote(like, like, sem, sem, sibling).wait_send()

    pl.semaphore_wait(barrier, len(peers))

    for k in (2, 1, 3):
        send(psi.at[x, c, 0], first.at[c, 0, y, x], near_s, near_r.at[k - 1], y_to(k))
    for k in (2, 1, 3):
        send(psi.at[:, c, 1], first.at[c, 1, :, y], whole_s, whole_r.at[k - 1], y_to(k))

    loads[0].wait()

    def split_right(j, carry):
        high, low = halves(right[j].T)
        right3[j, 0:N] = high
        right3[j, N : 2 * N] = high
        right3[j, 2 * N :] = low
        return carry

    lax.fori_loop(0, 4, split_right, 0)

    def forward(k, carry):
        here = first.at[c, 0, lax.rem(y + 4 - k, 4), x]
        arrived(here, near_r.at[k - 1])
        for m in (2, 1, 3):
            send(here, here, forward_s, forward_r.at[k - 1], x_to(m))
        return carry

    lax.fori_loop(1, 4, forward, 0)

    loads[1].wait()

    def split_left(j, carry):
        for cc in range(2):
            for xx in range(4):
                row = 96 * xx + 48 * cc
                high, low = halves(left[j, row : row + 48])
                rows = slice(48 * xx, 48 * xx + 48)
                left3[j, cc, rows, 0:N] = high
                left3[j, cc, rows, N : 2 * N] = high
                left3[j, cc, rows, 2 * N :] = low
        return carry

    lax.fori_loop(0, 4, split_left, 0)

    for load in loads[2:]:
        load.wait()

    def cross(k, carry):
        sector = lax.rem(y + 4 - k, 4)
        arrived(big_in.at[0, 0, 0], forward_r.at[k - 1])
        here = first.at[c, 0, sector]
        send(here, here, cross_s.at[STEPS], cross_r.at[STEPS], sibling)
        here = first.at[c, 1, :, sector]
        arrived(here, whole_r.at[k - 1])
        send(here, here, cross_s.at[STEPS], cross_r.at[STEPS], sibling)
        return carry

    lax.fori_loop(1, 4, cross, 0)
    arrived(big_in.at[0], cross_r.at[STEPS])

    count = pair_count[0]
    targets = [pair_out[0, j] for j in range(4)]

    def davidson_step(step, carry):
        vec = vecs.at[step]

        def convert(index, total):
            yy, xx = index // 4, lax.rem(index, 4)
            for cc in range(2):
                top = vec[cc, 0, yy, xx].reshape(24, N)
                bottom = vec[cc, 1, xx, yy].reshape(24, N)
                block = jnp.concatenate([top, bottom], axis=0)
                total = total + jnp.sum((block * block).reshape(6, 8, N), axis=0)
                high, low = halves(block)
                rows = pl.ds(pl.multiple_of(96 * xx + 48 * cc, 16), 48)
                vec3[yy, rows, 0:N] = high
                vec3[yy, rows, N : 2 * N] = low
                vec3[yy, rows, 2 * N :] = high
            return total

        squares = lax.fori_loop(0, 16, convert, jnp.zeros((8, N), F32))

        for j in range(4):
            high, low = halves(matmul(vec3[pair_in[0, j]], right3[j]))
            inner3[j, 0:N] = high
            inner3[j, N : 2 * N] = low
            inner3[j, 2 * N :] = high

        def combine(side, cls, q, p):
            xx, yy = (p, q) if cls == 0 else (q, p)
            rows = pl.ds(pl.multiple_of(48 * xx + 24 * cls, 8), 24)
            terms = []
            for j in range(4):
                live = jnp.logical_and(targets[j] == yy, count > j)
                terms.append(jnp.where(live, product[j, rows], 0.0))
            value = ((terms[0] + terms[1]) + (terms[2] + terms[3])).reshape(3, 8, N)
            return value, jnp.sum(value * vec[side, cls, q, p], axis=0)

        far, own = part_far.at[step], part_near.at[step]
        for j in range(4):
            product[j] = matmul(left3[j, d], inner3[j])

        def far_rows(i, dot):
            k = lax.rem(i + 1, 4)
            for cls in range(2):
                q = lax.rem(q_me[cls] + k, 4)
                for p in range(4):
                    value, term = combine(d, cls, q, p)
                    far[cls, q, p] = value
                    dot = dot + term
                send(
                    far.at[cls, q],
                    core_in.at[step, cls, q],
                    core_s.at[step],
                    core_r.at[step, cls, k],
                    sibling,
                )
            return dot

        dot = lax.fori_loop(0, 4, far_rows, jnp.zeros((8, N), F32))
        for j in range(4):
            product[j] = matmul(left3[j, c], inner3[j])

        def near_rows(i, dot):
            k = lax.rem(i + 1, 4)
            for cls in range(2):
                q = lax.rem(q_me[cls] + k, 4)
                arrived(core_in.at[step, cls, q], core_r.at[step, cls, k])
                for p in range(4):
                    value, term = combine(c, cls, q, p)
                    own[cls, q, p] = value + core_in[step, cls, q, p]
                    dot = dot + term
                for m in (2, 1, 3):
                    send(
                        own.at[cls, q, lax.rem(p_me[cls] + m, 4)],
                        big_in.at[step, cls, k, m - 1],
                        big_s.at[step],
                        big_r.at[step, cls, k],
                        p_to[cls](m),
                    )
            return dot

        dot = lax.fori_loop(0, 4, near_rows, dot)

        tiles = dots.at[step]
        tiles[c] = dot[:, 0:128] + dot[:, 128:256] + dot[:, 256:384]
        send(tiles.at[c], tiles.at[c], dot_s.at[step], dot_r.at[step, 0], sibling)
        arrived(tiles.at[0], dot_r.at[step, 0])
        tiles[2 + z] = tiles[0] + tiles[1]
        for k in (4, 3, 5, 2, 6, 1, 7):
            send(tiles.at[2 + z], tiles.at[2 + z], dot_s.at[step], dot_r.at[step, 1], z_to(k))

        mean_square = jnp.sum(squares, axis=(0, 1), keepdims=True) / CELLS + EPSILON
        inverse = 1.0 / jnp.sqrt(mean_square)

        def gathered(k):
            for cls in range(2):
                arrived(big_in.at[step, cls, k], big_r.at[step, cls, k])
                q = lax.rem(q_me[cls] + k, 4)
                value = own[cls, q, p_me[cls]] + big_in[step, cls, k, 0]
                mid[step, cls, q] = value + (big_in[step, cls, k, 1] + big_in[step, cls, k, 2])

        def small(k, carry):
            gathered(k)
            for cls in range(2):
                send(
                    mid.at[step, cls, lax.rem(q_me[cls] + k, 4)],
                    small_in.at[step, cls, k - 1],
                    small_s.at[step],
                    small_r.at[step, cls],
                    q_to[cls](k),
                )
            return carry

        lax.fori_loop(1, 4, small, 0)
        arrived(tiles.at[pl.ds(2, 7)], dot_r.at[step, 1])
        pairs = [tiles[2 + 2 * i] + tiles[3 + 2 * i] for i in range(4)]
        tiles[10 + x] = (pairs[0] + pairs[1]) + (pairs[2] + pairs[3])
        for k in (2, 1, 3):
            send(tiles.at[10 + x], tiles.at[10 + x], dot_s.at[step], dot_r.at[step, 2], x_to(k))
        gathered(0)
        arrived(tiles.at[pl.ds(10, 3)], dot_r.at[step, 2])
        tiles[14 + y] = (tiles[10] + tiles[11]) + (tiles[12] + tiles[13])
        for k in (2, 1, 3):
            send(tiles.at[14 + y], tiles.at[14 + y], dot_s.at[step], dot_r.at[step, 3], y_to(k))

        for cls in range(2):
            arrived(small_in.at[step, cls], small_r.at[step, cls])
            value = mid[step, cls, q_me[cls]] + small_in[step, cls, 0]
            last[step, cls] = value + (small_in[step, cls, 1] + small_in[step, cls, 2])
            for i in range(3):
                to = 3 * cls + i

                @pl.when(z != to)
                def _(to=to, cls=cls, i=i):
                    slot = lax.rem(to - z + 8, 8) - 1
                    send(
                        last.at[step, cls, i],
                        z_in.at[step, slot],
                        z_s.at[step],
                        z_r.at[step],
                        device(to, x, c, y),
                    )

        arrived(tiles.at[pl.ds(14, 3)], dot_r.at[step, 3])
        tile = (tiles[14] + tiles[15]) + (tiles[16] + tiles[17])
        rayleigh = jnp.sum(tile, axis=(0, 1), keepdims=True) * (inverse * inverse) / CELLS

        @pl.when(z < 6)
        def _():
            high, low = z // 3, lax.rem(z, 3)
            normed = fresh[step, high, low] * inverse
            scale = 1.0 / jnp.maximum(jnp.abs(diagonal_own[...] - rayleigh), 1.0)
            arrived(z_in.at[step], z_r.at[step])
            total = last[step, high, low] + z_in[step, 6]
            for i in (0, 2, 4):
                total = total + (z_in[step, i] + z_in[step, i + 1])
            residual = total * inverse - rayleigh * normed
            fresh[step + 1, high, low] = normed - residual * scale
            here = fresh.at[step + 1, high, low]
            for k in (4, 3, 5, 2, 6, 1, 7):
                send(here, here, owner_s.at[step], owner_r.at[step], z_to(k))
            arrived(z_in.at[step, pl.ds(0, 5)], owner_r.at[step])

        @pl.when(z >= 6)
        def _():
            arrived(z_in.at[step, pl.ds(0, 6)], owner_r.at[step])

        energies[step] = jnp.sum(rayleigh)

        @pl.when(step < STEPS - 1)
        def _():
            after = vecs.at[step + 1]
            for cls in range(2):
                here = fresh.at[step + 1, cls]
                there = after.at[c, cls, q_me[cls], p_me[cls]]
                for k in (2, 1, 3):
                    send(here, there, grow_s, grow_r.at[cls, k - 1], q_to[cls](k))
                for m in (2, 1, 3):
                    send(here, there, wide_s, wide_r.at[cls, 0], p_to[cls](m))
                after[c, cls, q_me[cls], p_me[cls]] = fresh[step + 1, cls]

            def grow(k, carry):
                for cls in range(2):
                    here = after.at[c, cls, lax.rem(q_me[cls] + 4 - k, 4), p_me[cls]]
                    arrived(here, grow_r.at[cls, k - 1])
                    for m in (2, 1, 3):
                        send(here, here, wide_s, wide_r.at[cls, k], p_to[cls](m))
                return carry

            lax.fori_loop(1, 4, grow, 0)

            def over(k, carry):
                for cls in range(2):
                    arrived(big_in.at[0, 0, 0], wide_r.at[cls, k])
                    here = after.at[c, cls, lax.rem(q_me[cls] + 4 - k, 4)]
                    send(here, here, cross_s.at[step], cross_r.at[step], sibling)
                return carry

            lax.fori_loop(0, 4, over, 0)
            arrived(after.at[d], cross_r.at[step])
            left_here(small_in.at[0], grow_s)
            left_here(big_in.at[0], wide_s)
            left_here(after.at[d], cross_s.at[step])

        @pl.when(step == STEPS - 1)
        def _():
            here = fresh.at[step + 1]
            for m in (2, 1, 3):
                send(here, out.at[x, c], end_s, end_r.at[m - 1], x_to(m))
            send(here, out.at[x, c], cross_s.at[step], cross_r.at[step], sibling)
            out[x, c] = fresh[step + 1]

            def over(m, carry):
                here = out.at[lax.rem(x + 4 - m, 4), c]
                arrived(here, end_r.at[m - 1])
                send(here, here, cross_s.at[step], cross_r.at[step], sibling)
                return carry

            lax.fori_loop(1, 4, over, 0)
            arrived(out.at[:, d], cross_r.at[step])
            left_here(small_in.at[0], end_s)
            left_here(out.at[:, d], cross_s.at[step])

        left_here(part_far.at[0], core_s.at[step])
        left_here(big_in.at[0], big_s.at[step])
        left_here(small_in.at[0], small_s.at[step])
        left_here(tiles.at[pl.ds(0, 14)], dot_s.at[step])

        @pl.when(z < 6)
        def _():
            left_here(z_in.at[step, pl.ds(0, 5)], z_s.at[step])
            left_here(z_in.at[step], owner_s.at[step])

        @pl.when(z >= 6)
        def _():
            left_here(z_in.at[step, pl.ds(0, 6)], z_s.at[step])

        return carry

    lax.fori_loop(0, STEPS, davidson_step, 0)

    left_here(big_in.at[0, 0, 0], near_s)
    left_here(part_far.at[0, 0, pl.ds(0, 3)], whole_s)
    left_here(big_in.at[0, 0, pl.ds(0, 3)], forward_s)
    left_here(big_in.at[0], cross_s.at[STEPS])


def shards(psi_start, diagonal, left_ops, right_ops, pair_in, pair_out, pair_count):
    vmem = pl.BlockSpec(memory_space=pltpu.VMEM)
    smem = pl.BlockSpec(memory_space=pltpu.SMEM)
    hbm = pl.BlockSpec(memory_space=pltpu.HBM)
    dma = pltpu.SemaphoreType.DMA
    rows = (3, 8, N)
    blocks = (4, 2, 2, *rows)
    pieces = (2, 4, 4, *rows)
    psi, energies = pl.pallas_call(
        kernel,
        out_shape=(
            jax.ShapeDtypeStruct(blocks, F32),
            jax.ShapeDtypeStruct((STEPS,), F32),
        ),
        in_specs=[hbm] * 7,
        out_specs=(vmem, smem),
        scratch_shapes=[
            pltpu.SMEM((1, 4), jnp.int32),
            pltpu.SMEM((1, 4), jnp.int32),
            pltpu.SMEM((1,), jnp.int32),
            pltpu.VMEM((8, N), F32),
            pltpu.VMEM((4, N, N), F32),
            pltpu.VMEM((4, N, N), F32),
            pltpu.VMEM((4, 2, N // 2, 3 * N), BF16),
            pltpu.VMEM((4, 3 * N, N), BF16),
            pltpu.VMEM((4, N, 3 * N), BF16),
            pltpu.VMEM((4, 3 * N, N), BF16),
            pltpu.VMEM((4, N // 2, N), F32),
            pltpu.VMEM((STEPS, 2, *pieces), F32),
            pltpu.VMEM((STEPS, *pieces), F32),
            pltpu.VMEM((STEPS, *pieces), F32),
            pltpu.VMEM((STEPS, *pieces), F32),
            pltpu.VMEM((STEPS, 2, 4, 3, *rows), F32),
            pltpu.VMEM((STEPS, 2, 4, *rows), F32),
            pltpu.VMEM((STEPS, 2, 3, *rows), F32),
            pltpu.VMEM((STEPS, 2, *rows), F32),
            pltpu.VMEM((STEPS, 7, 8, N), F32),
            pltpu.VMEM((STEPS + 1, 2, *rows), F32),
            pltpu.VMEM((STEPS, 18, 8, 128), F32),
            dma((11,)),
            dma,
            dma((3,)),
            dma,
            dma((3,)),
            dma,
            dma((3,)),
            dma((STEPS,)),
            dma((STEPS, 2, 4)),
            dma((STEPS,)),
            dma((STEPS, 2, 4)),
            dma((STEPS,)),
            dma((STEPS, 2)),
            dma((STEPS,)),
            dma((STEPS,)),
            dma((STEPS,)),
            dma((STEPS,)),
            dma,
            dma((2, 3)),
            dma,
            dma((2, 4)),
            dma((STEPS + 1,)),
            dma((STEPS + 1,)),
            dma,
            dma((3,)),
            dma((STEPS,)),
            dma((STEPS, 4)),
        ],
        compiler_params=pltpu.CompilerParams(
            collective_id=0, has_side_effects=True, vmem_limit_bytes=60 * 1024 * 1024
        ),
    )(
        pair_in,
        pair_out,
        pair_count,
        psi_start.reshape(blocks),
        diagonal.reshape(blocks),
        left_ops,
        right_ops,
    )
    return psi.reshape(1, N, N), energies


def solution(mesh):
    both = ("term", "sector")
    in_specs = (
        P("sector", None, None),
        P("sector", None, None),
        P(both, None, None),
        P(both, None, None),
        P(both, None),
        P(both, None),
        P(both),
    )
    out_specs = (P("sector", None, None), P())
    return jax.shard_map(
        shards, mesh=mesh, in_specs=in_specs, out_specs=out_specs, check_vma=False
    )
```

```python
import functools

import jax
import jax.numpy as jnp
from jax import lax
from jax.experimental import pallas as pl
from jax.experimental.pallas import tpu as pltpu
from jax.sharding import PartitionSpec as P

STEPS = 2
EPSILON = 1e-06
N = 384
CELLS = float(4 * N * N)
F32 = jnp.float32
BF16 = jnp.bfloat16


def matmul(a, b):
    return lax.dot_general(a, b, (((1,), (0,)), ((), ())), preferred_element_type=F32)


def halves(value):
    high = value.astype(BF16)
    return high, (value - high.astype(F32)).astype(BF16)


def kernel(
    pair_in_hbm,
    pair_out_hbm,
    pair_count_hbm,
    psi,
    diagonal,
    left_hbm,
    right_hbm,
    out,
    energies,
    pair_in,
    pair_out,
    pair_count,
    diagonal_own,
    left,
    right,
    left3,
    right3,
    vec3,
    inner3,
    product,
    vecs,
    part_far,
    part_near,
    core_in,
    big_in,
    mid,
    small_in,
    last,
    z_in,
    fresh,
    dots,
    load_sem,
    near_s,
    near_r,
    whole_s,
    whole_r,
    forward_s,
    forward_r,
    core_s,
    core_r,
    big_s,
    big_r,
    small_s,
    small_r,
    z_s,
    z_r,
    owner_s,
    owner_r,
    grow_s,
    grow_r,
    wide_s,
    wide_r,
    cross_s,
    cross_r,
    end_s,
    end_r,
    dot_s,
    dot_r,
):
    t = lax.axis_index("term")
    y = lax.axis_index("sector")
    z = t // 8
    x = lax.rem(t // 2, 4)
    c = lax.rem(t, 2)
    d = 1 - c

    def device(z_, x_, c_, y_):
        return ((z_ * 4 + x_) * 2 + c_, y_)

    def x_to(k):
        return device(z, lax.rem(x + k, 4), c, y)

    def y_to(k):
        return device(z, x, c, lax.rem(y + k, 4))

    def z_to(k):
        return device(lax.rem(z + k, 8), x, c, y)

    sibling = device(z, x, d, y)

    p_me, q_me = (x, y), (y, x)
    p_to, q_to = (x_to, y_to), (y_to, x_to)

    barrier = pltpu.get_barrier_semaphore()
    peers = [z_to(k) for k in (4, 3, 5, 2, 6, 1, 7)]
    peers += [x_to(k) for k in (2, 1, 3)]
    peers += [y_to(k) for k in (2, 1, 3)]
    peers += [sibling]
    for peer in peers:
        pl.semaphore_signal(barrier, inc=1, device_id=peer, device_id_type=pl.DeviceIdType.MESH)

    first = vecs.at[0]
    owner = jnp.minimum(z, 5)
    copies = [
        (right_hbm, right),
        (left_hbm, left),
        (psi.at[x, c, owner // 3, lax.rem(owner, 3)], fresh.at[0, owner // 3, lax.rem(owner, 3)]),
        (diagonal.at[x, c, owner // 3, lax.rem(owner, 3)], diagonal_own),
        (pair_in_hbm, pair_in),
        (pair_out_hbm, pair_out),
        (pair_count_hbm, pair_count),
    ]
    for cc in range(2):
        for b in range(3):
            copies.append((psi.at[:, cc, 0, b], first.at[cc, 0, b, :, y]))
            copies.append((psi.at[:, cc, 1, b], first.at[cc, 1, b, y]))
    loads = []
    for source, target in copies:
        load = pltpu.make_async_copy(source, target, load_sem.at[len(loads)])
        load.start()
        loads.append(load)

    def remote(source, target, send_sem, recv_sem, peer):
        return pltpu.make_async_remote_copy(
            src_ref=source,
            dst_ref=target,
            send_sem=send_sem,
            recv_sem=recv_sem,
            device_id=peer,
            device_id_type=pl.DeviceIdType.MESH,
        )

    def send(source, target, send_sem, recv_sem, peer):
        remote(source, target, send_sem, recv_sem, peer).start()

    def arrived(like, sem):
        remote(like, like, sem, sem, sibling).wait_recv()

    def left_here(like, sem):
        remote(like, like, sem, sem, sibling).wait_send()

    pl.semaphore_wait(barrier, len(peers))

    for k in (2, 1, 3):
        send(psi.at[x, c, 0], first.at[c, 0, :, x, y], near_s, near_r.at[k - 1], y_to(k))
    for b in range(3):
        for k in (2, 1, 3):
            send(psi.at[:, c, 1, b], first.at[c, 1, b, y], whole_s, whole_r.at[k - 1], y_to(k))

    loads[0].wait()

    def split_right(j, carry):
        high, low = halves(right[j].T)
        right3[j, 0:N] = high
        right3[j, N : 2 * N] = high
        right3[j, 2 * N :] = low
        return carry

    lax.fori_loop(0, 4, split_right, 0)

    def forward(k, carry):
        here = first.at[c, 0, :, x, lax.rem(y + 4 - k, 4)]
        arrived(here, near_r.at[k - 1])
        for m in (2, 1, 3):
            send(here, here, forward_s, forward_r.at[k - 1], x_to(m))
        return carry

    lax.fori_loop(1, 4, forward, 0)

    loads[1].wait()

    def split_left(j, carry):
        for cc in range(2):
            for xx in range(4):
                row = 96 * xx + 48 * cc
                high, low = halves(left[j, row : row + 48])
                rows = slice(48 * xx, 48 * xx + 48)
                left3[j, cc, rows, 0:N] = high
                left3[j, cc, rows, N : 2 * N] = high
                left3[j, cc, rows, 2 * N :] = low
        return carry

    lax.fori_loop(0, 4, split_left, 0)

    for load in loads[2:]:
        load.wait()

    def cross(k, carry):
        sector = lax.rem(y + 4 - k, 4)
        arrived(small_in.at[0, 0], forward_r.at[k - 1])
        here = first.at[c, 0, :, :, sector]
        send(here, here, cross_s.at[STEPS], cross_r.at[STEPS], sibling)
        arrived(big_in.at[0, 0, 0], whole_r.at[k - 1])
        here = first.at[c, 1, :, sector]
        send(here, here, cross_s.at[STEPS], cross_r.at[STEPS], sibling)
        return carry

    lax.fori_loop(1, 4, cross, 0)
    arrived(big_in.at[0], cross_r.at[STEPS])

    count = pair_count[0]
    live = [
        [jnp.logical_and(pair_out[0, j] == yy, count > j) for yy in range(4)] for j in range(4)
    ]

    def davidson_step(step, carry):
        vec = vecs.at[step]

        def convert(index, total):
            yy, xx = index // 4, lax.rem(index, 4)
            for cc in range(2):
                top = vec[cc, 0, :, xx, yy].reshape(24, N)
                bottom = vec[cc, 1, :, yy, xx].reshape(24, N)
                block = jnp.concatenate([top, bottom], axis=0)
                total = total + jnp.sum((block * block).reshape(6, 8, N), axis=0)
                high, low = halves(block)
                rows = pl.ds(pl.multiple_of(96 * xx + 48 * cc, 16), 48)
                vec3[yy, rows, 0:N] = high
                vec3[yy, rows, N : 2 * N] = low
                vec3[yy, rows, 2 * N :] = high
            return total

        squares = lax.fori_loop(0, 16, convert, jnp.zeros((8, N), F32))

        for j in range(4):
            high, low = halves(matmul(vec3[pair_in[0, j]], right3[j]))
            inner3[j, 0:N] = high
            inner3[j, N : 2 * N] = low
            inner3[j, 2 * N :] = high

        def combine(side, cls, b, store, dot):
            for xx in range(4):
                rows = pl.ds(pl.multiple_of(48 * xx + 24 * cls + 8 * b, 8), 8)
                blocks = [product[j, rows] for j in range(4)]
                for yy in range(4):
                    p, q = (xx, yy) if cls == 0 else (yy, xx)
                    terms = [jnp.where(live[j][yy], blocks[j], 0.0) for j in range(4)]
                    value = (terms[0] + terms[1]) + (terms[2] + terms[3])
                    store(p, q, value)
                    dot = dot + value * vec[side, cls, b, p, q]
            return dot

        far, own = part_far.at[step], part_near.at[step]
        for j in range(4):
            product[j] = matmul(left3[j, d], inner3[j])

        def far_rows(b, dot):
            for cls in range(2):

                def store(p, q, value, cls=cls):
                    far[cls, b, p, q] = value

                dot = combine(d, cls, b, store, dot)
                send(
                    far.at[cls, b],
                    core_in.at[step, cls, b],
                    core_s.at[step],
                    core_r.at[step, cls, b],
                    sibling,
                )
            return dot

        dot = lax.fori_loop(0, 3, far_rows, jnp.zeros((8, N), F32))
        for j in range(4):
            product[j] = matmul(left3[j, c], inner3[j])

        def near_rows(b, dot):
            for cls in range(2):
                arrived(core_in.at[step, cls, b], core_r.at[step, cls, b])

                def store(p, q, value, cls=cls):
                    own[cls, b, p, q] = value + core_in[step, cls, b, p, q]

                dot = combine(c, cls, b, store, dot)
                for m in (2, 1, 3):
                    send(
                        own.at[cls, b, lax.rem(p_me[cls] + m, 4)],
                        big_in.at[step, cls, b, m - 1],
                        big_s.at[step],
                        big_r.at[step, cls, b],
                        p_to[cls](m),
                    )
            return dot

        dot = lax.fori_loop(0, 3, near_rows, dot)

        tiles = dots.at[step]
        tiles[c] = dot[:, 0:128] + dot[:, 128:256] + dot[:, 256:384]
        send(tiles.at[c], tiles.at[c], dot_s.at[step], dot_r.at[step, 0], sibling)
        arrived(tiles.at[0], dot_r.at[step, 0])
        tiles[2 + z] = tiles[0] + tiles[1]
        for k in (4, 3, 5, 2, 6, 1, 7):
            send(tiles.at[2 + z], tiles.at[2 + z], dot_s.at[step], dot_r.at[step, 1], z_to(k))

        mean_square = jnp.sum(squares, axis=(0, 1), keepdims=True) / CELLS + EPSILON
        inverse = 1.0 / jnp.sqrt(mean_square)

        def small(b):
            for cls in range(2):
                arrived(big_in.at[step, cls, b], big_r.at[step, cls, b])
                value = own[cls, b, p_me[cls]] + big_in[step, cls, b, 0]
                value = value + (big_in[step, cls, b, 1] + big_in[step, cls, b, 2])
                mid[step, cls, b] = value
                for k in (2, 1, 3):
                    send(
                        mid.at[step, cls, b, lax.rem(q_me[cls] + k, 4)],
                        small_in.at[step, cls, b, k - 1],
                        small_s.at[step],
                        small_r.at[step, cls, b],
                        q_to[cls](k),
                    )

        def to_owner(b):
            for cls in range(2):
                arrived(small_in.at[step, cls, b], small_r.at[step, cls, b])
                value = mid[step, cls, b, q_me[cls]] + small_in[step, cls, b, 0]
                last[step, cls, b] = value + (small_in[step, cls, b, 1] + small_in[step, cls, b, 2])
                to = 3 * cls + b

                @pl.when(z != to)
                def _(to=to, cls=cls):
                    send(
                        last.at[step, cls, b],
                        z_in.at[step, lax.rem(to - z + 8, 8) - 1],
                        z_s.at[step],
                        z_r.at[step],
                        device(to, x, c, y),
                    )

        def update(b, rayleigh):
            @pl.when(jnp.logical_or(z == b, z == b + 3))
            def _():
                high = z // 3
                normed = fresh[step, high, b] * inverse
                scale = 1.0 / jnp.maximum(jnp.abs(diagonal_own[...] - rayleigh), 1.0)
                arrived(z_in.at[step], z_r.at[step])
                total = last[step, high, b] + z_in[step, 6]
                for i in (0, 2, 4):
                    total = total + (z_in[step, i] + z_in[step, i + 1])
                residual = total * inverse - rayleigh * normed
                fresh[step + 1, high, b] = normed - residual * scale
                here = fresh.at[step + 1, high, b]
                for k in (4, 3, 5, 2, 6, 1, 7):
                    send(here, here, owner_s.at[step], owner_r.at[step, b], z_to(k))

        def from_owners(b):
            mine = jnp.logical_or(z == b, z == b + 3)

            @pl.when(mine)
            def _():
                arrived(z_in.at[step, pl.ds(0, 1)], owner_r.at[step, b])

            @pl.when(jnp.logical_not(mine))
            def _():
                arrived(z_in.at[step, pl.ds(0, 2)], owner_r.at[step, b])

        small(0)
        arrived(tiles.at[pl.ds(2, 7)], dot_r.at[step, 1])
        pairs = [tiles[2 + 2 * i] + tiles[3 + 2 * i] for i in range(4)]
        tiles[10 + x] = (pairs[0] + pairs[1]) + (pairs[2] + pairs[3])
        for k in (2, 1, 3):
            send(tiles.at[10 + x], tiles.at[10 + x], dot_s.at[step], dot_r.at[step, 2], x_to(k))
        small(1)
        to_owner(0)
        arrived(tiles.at[pl.ds(10, 3)], dot_r.at[step, 2])
        tiles[14 + y] = (tiles[10] + tiles[11]) + (tiles[12] + tiles[13])
        for k in (2, 1, 3):
            send(tiles.at[14 + y], tiles.at[14 + y], dot_s.at[step], dot_r.at[step, 3], y_to(k))
        small(2)
        to_owner(1)
        arrived(tiles.at[pl.ds(14, 3)], dot_r.at[step, 3])
        tile = (tiles[14] + tiles[15]) + (tiles[16] + tiles[17])
        rayleigh = jnp.sum(tile, axis=(0, 1), keepdims=True) * (inverse * inverse) / CELLS
        update(0, rayleigh)
        to_owner(2)
        energies[step] = jnp.sum(rayleigh)
        update(1, rayleigh)

        @pl.when(step < STEPS - 1)
        def _():
            after = vecs.at[step + 1]

            def grow(b):
                from_owners(b)
                for cls in range(2):
                    here = fresh.at[step + 1, cls, b]
                    there = after.at[c, cls, b, p_me[cls], q_me[cls]]
                    for k in (2, 1, 3):
                        send(here, there, grow_s, grow_r.at[cls, b], q_to[cls](k))
                    after[c, cls, b, p_me[cls], q_me[cls]] = fresh[step + 1, cls, b]

            def wide(b):
                for cls in range(2):
                    arrived(small_in.at[0, 0, 0], grow_r.at[cls, b])
                    here = after.at[c, cls, b, p_me[cls]]
                    for m in (2, 1, 3):
                        send(here, here, wide_s, wide_r.at[cls, b], p_to[cls](m))

            def over(b):
                for cls in range(2):
                    arrived(big_in.at[0, 0, 0], wide_r.at[cls, b])
                    here = after.at[c, cls, b]
                    send(here, here, cross_s.at[step], cross_r.at[step], sibling)

            grow(0)
            update(2, rayleigh)
            wide(0)
            grow(1)
            grow(2)
            wide(1)
            over(0)
            wide(2)
            over(1)
            over(2)
            arrived(after.at[d], cross_r.at[step])
            left_here(small_in.at[0], grow_s)
            left_here(big_in.at[0], wide_s)
            left_here(after.at[d], cross_s.at[step])

        @pl.when(step == STEPS - 1)
        def _():
            def grow(b):
                from_owners(b)
                here, there = fresh.at[step + 1, :, b], out.at[x, c, :, b]
                for m in (2, 1, 3):
                    send(here, there, end_s, end_r.at[b], x_to(m))
                out[x, c, :, b] = fresh[step + 1, :, b]

            def over(b):
                arrived(small_in.at[0, 0, pl.ds(0, 2)], end_r.at[b])
                here = out.at[:, c, :, b]
                send(here, here, cross_s.at[step], cross_r.at[step], sibling)

            grow(0)
            update(2, rayleigh)
            grow(1)
            over(0)
            grow(2)
            over(1)
            over(2)
            arrived(out.at[:, d], cross_r.at[step])
            left_here(small_in.at[0], end_s)
            left_here(out.at[:, d], cross_s.at[step])

        left_here(part_far.at[0], core_s.at[step])
        left_here(big_in.at[0], big_s.at[step])
        left_here(small_in.at[0], small_s.at[step])
        left_here(tiles.at[pl.ds(0, 14)], dot_s.at[step])

        @pl.when(z < 6)
        def _():
            left_here(z_in.at[step, pl.ds(0, 5)], z_s.at[step])
            left_here(z_in.at[step], owner_s.at[step])

        @pl.when(z >= 6)
        def _():
            left_here(z_in.at[step, pl.ds(0, 6)], z_s.at[step])

        return carry

    lax.fori_loop(0, STEPS, davidson_step, 0)

    left_here(small_in.at[0, 0], near_s)
    left_here(big_in.at[0, 0], whole_s)
    left_here(part_far.at[0, 0, :, pl.ds(0, 3), pl.ds(0, 3)], forward_s)
    left_here(big_in.at[0], cross_s.at[STEPS])


def shards(psi_start, diagonal, left_ops, right_ops, pair_in, pair_out, pair_count):
    vmem = pl.BlockSpec(memory_space=pltpu.VMEM)
    smem = pl.BlockSpec(memory_space=pltpu.SMEM)
    hbm = pl.BlockSpec(memory_space=pltpu.HBM)
    dma = pltpu.SemaphoreType.DMA
    rows = (3, 8, N)
    blocks = (4, 2, 2, *rows)
    pieces = (2, 3, 4, 4, 8, N)
    psi, energies = pl.pallas_call(
        kernel,
        out_shape=(
            jax.ShapeDtypeStruct(blocks, F32),
            jax.ShapeDtypeStruct((STEPS,), F32),
        ),
        in_specs=[hbm] * 7,
        out_specs=(vmem, smem),
        scratch_shapes=[
            pltpu.SMEM((1, 4), jnp.int32),
            pltpu.SMEM((1, 4), jnp.int32),
            pltpu.SMEM((1,), jnp.int32),
            pltpu.VMEM((8, N), F32),
            pltpu.VMEM((4, N, N), F32),
            pltpu.VMEM((4, N, N), F32),
            pltpu.VMEM((4, 2, N // 2, 3 * N), BF16),
            pltpu.VMEM((4, 3 * N, N), BF16),
            pltpu.VMEM((4, N, 3 * N), BF16),
            pltpu.VMEM((4, 3 * N, N), BF16),
            pltpu.VMEM((4, N // 2, N), F32),
            pltpu.VMEM((STEPS, 2, *pieces), F32),
            pltpu.VMEM((STEPS, *pieces), F32),
            pltpu.VMEM((STEPS, *pieces), F32),
            pltpu.VMEM((STEPS, *pieces), F32),
            pltpu.VMEM((STEPS, 2, 3, 3, 4, 8, N), F32),
            pltpu.VMEM((STEPS, 2, 3, 4, 8, N), F32),
            pltpu.VMEM((STEPS, 2, 3, 3, 8, N), F32),
            pltpu.VMEM((STEPS, 2, *rows), F32),
            pltpu.VMEM((STEPS, 7, 8, N), F32),
            pltpu.VMEM((STEPS + 1, 2, *rows), F32),
            pltpu.VMEM((STEPS, 18, 8, 128), F32),
            dma((19,)),
            dma,
            dma((3,)),
            dma,
            dma((3,)),
            dma,
            dma((3,)),
            dma((STEPS,)),
            dma((STEPS, 2, 3)),
            dma((STEPS,)),
            dma((STEPS, 2, 3)),
            dma((STEPS,)),
            dma((STEPS, 2, 3)),
            dma((STEPS,)),
            dma((STEPS,)),
            dma((STEPS,)),
            dma((STEPS, 3)),
            dma,
            dma((2, 3)),
            dma,
            dma((2, 3)),
            dma((STEPS + 1,)),
            dma((STEPS + 1,)),
            dma,
            dma((3,)),
            dma((STEPS,)),
            dma((STEPS, 4)),
        ],
        compiler_params=pltpu.CompilerParams(
            collective_id=0, has_side_effects=True, vmem_limit_bytes=60 * 1024 * 1024
        ),
    )(
        pair_in,
        pair_out,
        pair_count,
        psi_start.reshape(blocks),
        diagonal.reshape(blocks),
        left_ops,
        right_ops,
    )
    return psi.reshape(1, N, N), energies


def solution(mesh):
    both = ("term", "sector")
    in_specs = (
        P("sector", None, None),
        P("sector", None, None),
        P(both, None, None),
        P(both, None, None),
        P(both, None),
        P(both, None),
        P(both),
    )
    out_specs = (P("sector", None, None), P())
    return jax.shard_map(
        shards, mesh=mesh, in_specs=in_specs, out_specs=out_specs, check_vma=False
    )
```

```python
import functools

import jax
import jax.numpy as jnp
from jax import lax
from jax.experimental import pallas as pl
from jax.experimental.pallas import tpu as pltpu
from jax.sharding import PartitionSpec as P

STEPS = 2
EPSILON = 1e-06
N = 384
CELLS = float(4 * N * N)
F32 = jnp.float32
BF16 = jnp.bfloat16


def matmul(a, b):
    return lax.dot_general(a, b, (((1,), (0,)), ((), ())), preferred_element_type=F32)


def halves(value):
    high = value.astype(BF16)
    return high, (value - high.astype(F32)).astype(BF16)


def kernel(
    pair_in_hbm,
    pair_out_hbm,
    pair_count_hbm,
    psi,
    diagonal,
    left_hbm,
    right_hbm,
    out,
    energies,
    pair_in,
    pair_out,
    pair_count,
    diagonal_own,
    left,
    right,
    left3,
    right3,
    vec3,
    inner3,
    product,
    vecs,
    part_far,
    part_near,
    core_in,
    big_in,
    mid,
    small_in,
    last,
    z_in,
    fresh,
    dots,
    load_sem,
    near_s,
    near_r,
    whole_s,
    whole_r,
    forward_s,
    forward_r,
    core_s,
    core_r,
    big_s,
    big_r,
    small_s,
    small_r,
    z_s,
    z_r,
    owner_s,
    owner_r,
    grow_s,
    grow_r,
    wide_s,
    wide_r,
    cross_s,
    cross_r,
    end_s,
    end_r,
    dot_s,
    dot_r,
):
    t = lax.axis_index("term")
    y = lax.axis_index("sector")
    z = t // 8
    x = lax.rem(t // 2, 4)
    c = lax.rem(t, 2)
    d = 1 - c

    def device(z_, x_, c_, y_):
        return ((z_ * 4 + x_) * 2 + c_, y_)

    def x_to(k):
        return device(z, lax.rem(x + k, 4), c, y)

    def y_to(k):
        return device(z, x, c, lax.rem(y + k, 4))

    def z_to(k):
        return device(lax.rem(z + k, 8), x, c, y)

    sibling = device(z, x, d, y)

    p_me, q_me = (x, y), (y, x)
    p_to, q_to = (x_to, y_to), (y_to, x_to)

    barrier = pltpu.get_barrier_semaphore()
    peers = [z_to(k) for k in (4, 3, 5, 2, 6, 1, 7)]
    peers += [x_to(k) for k in (2, 1, 3)]
    peers += [y_to(k) for k in (2, 1, 3)]
    peers += [sibling]
    for peer in peers:
        pl.semaphore_signal(barrier, inc=1, device_id=peer, device_id_type=pl.DeviceIdType.MESH)

    first = vecs.at[0]
    owner = jnp.minimum(z, 5)
    copies = [
        (right_hbm, right),
        (left_hbm, left),
        (psi.at[x, c, owner // 3, lax.rem(owner, 3)], fresh.at[0, owner // 3, lax.rem(owner, 3)]),
        (diagonal.at[x, c, owner // 3, lax.rem(owner, 3)], diagonal_own),
        (pair_in_hbm, pair_in),
        (pair_out_hbm, pair_out),
        (pair_count_hbm, pair_count),
    ]
    for cc in range(2):
        for b in range(3):
            copies.append((psi.at[:, cc, 0, b], first.at[cc, 0, b, :, y]))
            copies.append((psi.at[:, cc, 1, b], first.at[cc, 1, b, y]))
    loads = []
    for source, target in copies:
        load = pltpu.make_async_copy(source, target, load_sem.at[len(loads)])
        load.start()
        loads.append(load)

    def remote(source, target, send_sem, recv_sem, peer):
        return pltpu.make_async_remote_copy(
            src_ref=source,
            dst_ref=target,
            send_sem=send_sem,
            recv_sem=recv_sem,
            device_id=peer,
            device_id_type=pl.DeviceIdType.MESH,
        )

    def send(source, target, send_sem, recv_sem, peer):
        remote(source, target, send_sem, recv_sem, peer).start()

    def arrived(like, sem):
        remote(like, like, sem, sem, sibling).wait_recv()

    def left_here(like, sem):
        remote(like, like, sem, sem, sibling).wait_send()

    pl.semaphore_wait(barrier, len(peers))

    for k in (2, 1, 3):
        send(psi.at[x, c, 0], first.at[c, 0, :, x, y], near_s, near_r.at[k - 1], y_to(k))
    for b in range(3):
        for k in (2, 1, 3):
            send(psi.at[:, c, 1, b], first.at[c, 1, b, y], whole_s, whole_r.at[k - 1], y_to(k))

    loads[0].wait()

    def split_right(j, carry):
        high, low = halves(right[j].T)
        right3[j, 0:N] = high
        right3[j, N : 2 * N] = high
        right3[j, 2 * N :] = low
        return carry

    lax.fori_loop(0, 4, split_right, 0)

    def forward(k, carry):
        here = first.at[c, 0, :, x, lax.rem(y + 4 - k, 4)]
        arrived(here, near_r.at[k - 1])
        for m in (2, 1, 3):
            send(here, here, forward_s, forward_r.at[k - 1], x_to(m))
        return carry

    lax.fori_loop(1, 4, forward, 0)

    loads[1].wait()

    def split_left(j, carry):
        for cc in range(2):
            for xx in range(4):
                row = 96 * xx + 48 * cc
                high, low = halves(left[j, row : row + 48])
                rows = slice(48 * xx, 48 * xx + 48)
                left3[j, cc, rows, 0:N] = high
                left3[j, cc, rows, N : 2 * N] = high
                left3[j, cc, rows, 2 * N :] = low
        return carry

    lax.fori_loop(0, 4, split_left, 0)

    for load in loads[2:]:
        load.wait()

    def cross(k, carry):
        sector = lax.rem(y + 4 - k, 4)
        arrived(small_in.at[0, 0], forward_r.at[k - 1])
        here = first.at[c, 0, :, :, sector]
        send(here, here, cross_s.at[STEPS], cross_r.at[STEPS], sibling)
        arrived(big_in.at[0, 0, 0], whole_r.at[k - 1])
        here = first.at[c, 1, :, sector]
        send(here, here, cross_s.at[STEPS], cross_r.at[STEPS], sibling)
        return carry

    lax.fori_loop(1, 4, cross, 0)
    arrived(big_in.at[0], cross_r.at[STEPS])

    count = pair_count[0]
    live = [
        [jnp.logical_and(pair_out[0, j] == yy, count > j) for yy in range(4)] for j in range(4)
    ]

    def davidson_step(step, carry):
        vec = vecs.at[step]

        def convert(index, total):
            yy, xx = index // 4, lax.rem(index, 4)
            for cc in range(2):
                top = vec[cc, 0, :, xx, yy].reshape(24, N)
                bottom = vec[cc, 1, :, yy, xx].reshape(24, N)
                block = jnp.concatenate([top, bottom], axis=0)
                total = total + jnp.sum((block * block).reshape(6, 8, N), axis=0)
                high, low = halves(block)
                rows = pl.ds(pl.multiple_of(96 * xx + 48 * cc, 16), 48)
                vec3[yy, rows, 0:N] = high
                vec3[yy, rows, N : 2 * N] = low
                vec3[yy, rows, 2 * N :] = high
            return total

        squares = lax.fori_loop(0, 16, convert, jnp.zeros((8, N), F32))

        for j in range(4):
            high, low = halves(matmul(vec3[pair_in[0, j]], right3[j]))
            inner3[j, 0:N] = high
            inner3[j, N : 2 * N] = low
            inner3[j, 2 * N :] = high

        def combine(side, cls, b, store, dot):
            for xx in range(4):
                rows = pl.ds(pl.multiple_of(48 * xx + 24 * cls + 8 * b, 8), 8)
                blocks = [product[j, rows] for j in range(4)]
                for yy in range(4):
                    p, q = (xx, yy) if cls == 0 else (yy, xx)
                    terms = [jnp.where(live[j][yy], blocks[j], 0.0) for j in range(4)]
                    value = (terms[0] + terms[1]) + (terms[2] + terms[3])
                    store(p, q, value)
                    dot = dot + value * vec[side, cls, b, p, q]
            return dot

        far, own = part_far.at[step], part_near.at[step]
        for j in range(4):
            product[j] = matmul(left3[j, d], inner3[j])

        def far_rows(b, dot):
            for cls in range(2):

                def store(p, q, value, cls=cls):
                    far[cls, b, p, q] = value

                dot = combine(d, cls, b, store, dot)
                send(
                    far.at[cls, b],
                    core_in.at[step, cls, b],
                    core_s.at[step],
                    core_r.at[step, cls, b],
                    sibling,
                )
            return dot

        dot = lax.fori_loop(0, 3, far_rows, jnp.zeros((8, N), F32))
        for j in range(4):
            product[j] = matmul(left3[j, c], inner3[j])

        def near_rows(b, dot):
            for cls in range(2):
                arrived(core_in.at[step, cls, b], core_r.at[step, cls, b])

                def store(p, q, value, cls=cls):
                    own[cls, b, p, q] = value + core_in[step, cls, b, p, q]

                dot = combine(c, cls, b, store, dot)
            return dot

        def large(b):
            if b:
                left_here(big_in.at[0, :, 0], big_s.at[step, b - 1])
            for cls in range(2):
                for m in (2, 1, 3):
                    send(
                        own.at[cls, b, lax.rem(p_me[cls] + m, 4)],
                        big_in.at[step, cls, b, m - 1],
                        big_s.at[step, b],
                        big_r.at[step, cls, b],
                        p_to[cls](m),
                    )

        dot = near_rows(0, dot)
        large(0)
        dot = lax.fori_loop(1, 3, near_rows, dot)

        tiles = dots.at[step]
        tiles[c] = dot[:, 0:128] + dot[:, 128:256] + dot[:, 256:384]
        send(tiles.at[c], tiles.at[c], dot_s.at[step], dot_r.at[step, 0], sibling)
        arrived(tiles.at[0], dot_r.at[step, 0])
        tiles[2 + z] = tiles[0] + tiles[1]
        for k in (4, 3, 5, 2, 6, 1, 7):
            send(tiles.at[2 + z], tiles.at[2 + z], dot_s.at[step], dot_r.at[step, 1], z_to(k))

        mean_square = jnp.sum(squares, axis=(0, 1), keepdims=True) / CELLS + EPSILON
        inverse = 1.0 / jnp.sqrt(mean_square)

        def small(b):
            for cls in range(2):
                arrived(big_in.at[step, cls, b], big_r.at[step, cls, b])
                value = own[cls, b, p_me[cls]] + big_in[step, cls, b, 0]
                value = value + (big_in[step, cls, b, 1] + big_in[step, cls, b, 2])
                mid[step, cls, b] = value
                for k in (2, 1, 3):
                    send(
                        mid.at[step, cls, b, lax.rem(q_me[cls] + k, 4)],
                        small_in.at[step, cls, b, k - 1],
                        small_s.at[step],
                        small_r.at[step, cls, b],
                        q_to[cls](k),
                    )

        def to_owner(b):
            for cls in range(2):
                arrived(small_in.at[step, cls, b], small_r.at[step, cls, b])
                value = mid[step, cls, b, q_me[cls]] + small_in[step, cls, b, 0]
                last[step, cls, b] = value + (small_in[step, cls, b, 1] + small_in[step, cls, b, 2])
                to = 3 * cls + b

                @pl.when(z != to)
                def _(to=to, cls=cls):
                    send(
                        last.at[step, cls, b],
                        z_in.at[step, lax.rem(to - z + 8, 8) - 1],
                        z_s.at[step],
                        z_r.at[step],
                        device(to, x, c, y),
                    )

        def update(b, rayleigh):
            @pl.when(jnp.logical_or(z == b, z == b + 3))
            def _():
                high = z // 3
                normed = fresh[step, high, b] * inverse
                scale = 1.0 / jnp.maximum(jnp.abs(diagonal_own[...] - rayleigh), 1.0)
                arrived(z_in.at[step], z_r.at[step])
                total = last[step, high, b] + z_in[step, 6]
                for i in (0, 2, 4):
                    total = total + (z_in[step, i] + z_in[step, i + 1])
                residual = total * inverse - rayleigh * normed
                fresh[step + 1, high, b] = normed - residual * scale
                here = fresh.at[step + 1, high, b]
                for k in (4, 3, 5, 2, 6, 1, 7):
                    send(here, here, owner_s.at[step], owner_r.at[step, b], z_to(k))

        def from_owners(b):
            mine = jnp.logical_or(z == b, z == b + 3)

            @pl.when(mine)
            def _():
                arrived(z_in.at[step, pl.ds(0, 1)], owner_r.at[step, b])

            @pl.when(jnp.logical_not(mine))
            def _():
                arrived(z_in.at[step, pl.ds(0, 2)], owner_r.at[step, b])

        large(1)
        small(0)
        arrived(tiles.at[pl.ds(2, 7)], dot_r.at[step, 1])
        pairs = [tiles[2 + 2 * i] + tiles[3 + 2 * i] for i in range(4)]
        tiles[10 + x] = (pairs[0] + pairs[1]) + (pairs[2] + pairs[3])
        for k in (2, 1, 3):
            send(tiles.at[10 + x], tiles.at[10 + x], dot_s.at[step], dot_r.at[step, 2], x_to(k))
        large(2)
        small(1)
        to_owner(0)
        arrived(tiles.at[pl.ds(10, 3)], dot_r.at[step, 2])
        tiles[14 + y] = (tiles[10] + tiles[11]) + (tiles[12] + tiles[13])
        for k in (2, 1, 3):
            send(tiles.at[14 + y], tiles.at[14 + y], dot_s.at[step], dot_r.at[step, 3], y_to(k))
        small(2)
        to_owner(1)
        arrived(tiles.at[pl.ds(14, 3)], dot_r.at[step, 3])
        tile = (tiles[14] + tiles[15]) + (tiles[16] + tiles[17])
        rayleigh = jnp.sum(tile, axis=(0, 1), keepdims=True) * (inverse * inverse) / CELLS
        update(0, rayleigh)
        to_owner(2)
        energies[step] = jnp.sum(rayleigh)
        update(1, rayleigh)

        @pl.when(step < STEPS - 1)
        def _():
            after = vecs.at[step + 1]

            def grow(b):
                from_owners(b)
                for cls in range(2):
                    here = fresh.at[step + 1, cls, b]
                    there = after.at[c, cls, b, p_me[cls], q_me[cls]]
                    for k in (2, 1, 3):
                        send(here, there, grow_s, grow_r.at[cls, b], q_to[cls](k))
                    after[c, cls, b, p_me[cls], q_me[cls]] = fresh[step + 1, cls, b]

            def wide(b):
                for cls in range(2):
                    arrived(small_in.at[0, 0, 0], grow_r.at[cls, b])
                    here = after.at[c, cls, b, p_me[cls]]
                    for m in (2, 1, 3):
                        send(here, here, wide_s.at[b], wide_r.at[cls, b], p_to[cls](m))

            def over(b):
                for cls in range(2):
                    arrived(big_in.at[0, 0, 0], wide_r.at[cls, b])
                    here = after.at[c, cls, b]
                    send(here, here, cross_s.at[step], cross_r.at[step], sibling)

            grow(0)
            update(2, rayleigh)
            grow(1)
            wide(0)
            grow(2)
            wide(1)
            wide(2)
            over(0)
            over(1)
            over(2)
            arrived(after.at[d], cross_r.at[step])
            left_here(small_in.at[0], grow_s)
            for b in range(3):
                left_here(big_in.at[0, :, 0], wide_s.at[b])
            left_here(after.at[d], cross_s.at[step])

        @pl.when(step == STEPS - 1)
        def _():
            def grow(b):
                from_owners(b)
                here, there = fresh.at[step + 1, :, b], out.at[x, c, :, b]
                for m in (2, 1, 3):
                    send(here, there, end_s, end_r.at[b], x_to(m))
                out[x, c, :, b] = fresh[step + 1, :, b]

            def over(b):
                arrived(small_in.at[0, 0, pl.ds(0, 2)], end_r.at[b])
                here = out.at[:, c, :, b]
                send(here, here, cross_s.at[step], cross_r.at[step], sibling)

            grow(0)
            update(2, rayleigh)
            grow(1)
            over(0)
            grow(2)
            over(1)
            over(2)
            arrived(out.at[:, d], cross_r.at[step])
            left_here(small_in.at[0], end_s)
            left_here(out.at[:, d], cross_s.at[step])

        left_here(part_far.at[0], core_s.at[step])
        left_here(big_in.at[0, :, 0], big_s.at[step, 2])
        left_here(small_in.at[0], small_s.at[step])
        left_here(tiles.at[pl.ds(0, 14)], dot_s.at[step])

        @pl.when(z < 6)
        def _():
            left_here(z_in.at[step, pl.ds(0, 5)], z_s.at[step])
            left_here(z_in.at[step], owner_s.at[step])

        @pl.when(z >= 6)
        def _():
            left_here(z_in.at[step, pl.ds(0, 6)], z_s.at[step])

        return carry

    lax.fori_loop(0, STEPS, davidson_step, 0)

    left_here(small_in.at[0, 0], near_s)
    left_here(big_in.at[0, 0], whole_s)
    left_here(part_far.at[0, 0, :, pl.ds(0, 3), pl.ds(0, 3)], forward_s)
    left_here(big_in.at[0], cross_s.at[STEPS])


def shards(psi_start, diagonal, left_ops, right_ops, pair_in, pair_out, pair_count):
    vmem = pl.BlockSpec(memory_space=pltpu.VMEM)
    smem = pl.BlockSpec(memory_space=pltpu.SMEM)
    hbm = pl.BlockSpec(memory_space=pltpu.HBM)
    dma = pltpu.SemaphoreType.DMA
    rows = (3, 8, N)
    blocks = (4, 2, 2, *rows)
    pieces = (2, 3, 4, 4, 8, N)
    psi, energies = pl.pallas_call(
        kernel,
        out_shape=(
            jax.ShapeDtypeStruct(blocks, F32),
            jax.ShapeDtypeStruct((STEPS,), F32),
        ),
        in_specs=[hbm] * 7,
        out_specs=(vmem, smem),
        scratch_shapes=[
            pltpu.SMEM((1, 4), jnp.int32),
            pltpu.SMEM((1, 4), jnp.int32),
            pltpu.SMEM((1,), jnp.int32),
            pltpu.VMEM((8, N), F32),
            pltpu.VMEM((4, N, N), F32),
            pltpu.VMEM((4, N, N), F32),
            pltpu.VMEM((4, 2, N // 2, 3 * N), BF16),
            pltpu.VMEM((4, 3 * N, N), BF16),
            pltpu.VMEM((4, N, 3 * N), BF16),
            pltpu.VMEM((4, 3 * N, N), BF16),
            pltpu.VMEM((4, N // 2, N), F32),
            pltpu.VMEM((STEPS, 2, *pieces), F32),
            pltpu.VMEM((STEPS, *pieces), F32),
            pltpu.VMEM((STEPS, *pieces), F32),
            pltpu.VMEM((STEPS, *pieces), F32),
            pltpu.VMEM((STEPS, 2, 3, 3, 4, 8, N), F32),
            pltpu.VMEM((STEPS, 2, 3, 4, 8, N), F32),
            pltpu.VMEM((STEPS, 2, 3, 3, 8, N), F32),
            pltpu.VMEM((STEPS, 2, *rows), F32),
            pltpu.VMEM((STEPS, 7, 8, N), F32),
            pltpu.VMEM((STEPS + 1, 2, *rows), F32),
            pltpu.VMEM((STEPS, 18, 8, 128), F32),
            dma((19,)),
            dma,
            dma((3,)),
            dma,
            dma((3,)),
            dma,
            dma((3,)),
            dma((STEPS,)),
            dma((STEPS, 2, 3)),
            dma((STEPS, 3)),
            dma((STEPS, 2, 3)),
            dma((STEPS,)),
            dma((STEPS, 2, 3)),
            dma((STEPS,)),
            dma((STEPS,)),
            dma((STEPS,)),
            dma((STEPS, 3)),
            dma,
            dma((2, 3)),
            dma((3,)),
            dma((2, 3)),
            dma((STEPS + 1,)),
            dma((STEPS + 1,)),
            dma,
            dma((3,)),
            dma((STEPS,)),
            dma((STEPS, 4)),
        ],
        compiler_params=pltpu.CompilerParams(
            collective_id=0, has_side_effects=True, vmem_limit_bytes=54400 * 1024
        ),
    )(
        pair_in,
        pair_out,
        pair_count,
        psi_start.reshape(blocks),
        diagonal.reshape(blocks),
        left_ops,
        right_ops,
    )
    return psi.reshape(1, N, N), energies


def solution(mesh):
    both = ("term", "sector")
    in_specs = (
        P("sector", None, None),
        P("sector", None, None),
        P(both, None, None),
        P(both, None, None),
        P(both, None),
        P(both, None),
        P(both),
    )
    out_specs = (P("sector", None, None), P())
    return jax.shard_map(
        shards, mesh=mesh, in_specs=in_specs, out_specs=out_specs, check_vma=False
    )
```

```python
import functools

import jax
import jax.numpy as jnp
from jax import lax
from jax.experimental import pallas as pl
from jax.experimental.pallas import tpu as pltpu
from jax.sharding import PartitionSpec as P

STEPS = 2
EPSILON = 1e-06
N = 384
CELLS = float(4 * N * N)
F32 = jnp.float32
BF16 = jnp.bfloat16


def matmul(a, b):
    return lax.dot_general(a, b, (((1,), (0,)), ((), ())), preferred_element_type=F32)


def halves(value):
    high = value.astype(BF16)
    return high, (value - high.astype(F32)).astype(BF16)


def kernel(
    pair_in_hbm,
    pair_out_hbm,
    pair_count_hbm,
    psi,
    diagonal,
    left_hbm,
    right_hbm,
    out,
    energies,
    pair_in,
    pair_out,
    pair_count,
    diagonal_own,
    left,
    right,
    left3,
    right3,
    vec3,
    inner3,
    product,
    vecs,
    part_far,
    part_near,
    core_in,
    big_in,
    mid,
    small_in,
    last,
    z_in,
    fresh,
    dots,
    load_sem,
    near_s,
    near_r,
    whole_s,
    whole_r,
    forward_s,
    forward_r,
    core_s,
    core_r,
    big_s,
    big_r,
    small_s,
    small_r,
    z_s,
    z_r,
    owner_s,
    owner_r,
    grow_s,
    grow_r,
    wide_s,
    wide_r,
    cross_s,
    cross_r,
    end_s,
    end_r,
    dot_s,
    dot_r,
):
    t = lax.axis_index("term")
    y = lax.axis_index("sector")
    z = t // 8
    x = lax.rem(t // 2, 4)
    c = lax.rem(t, 2)
    d = 1 - c

    def device(z_, x_, c_, y_):
        return ((z_ * 4 + x_) * 2 + c_, y_)

    def x_to(k):
        return device(z, lax.rem(x + k, 4), c, y)

    def y_to(k):
        return device(z, x, c, lax.rem(y + k, 4))

    def z_to(k):
        return device(lax.rem(z + k, 8), x, c, y)

    sibling = device(z, x, d, y)

    p_me, q_me = (x, y), (y, x)
    p_to, q_to = (x_to, y_to), (y_to, x_to)

    barrier = pltpu.get_barrier_semaphore()
    peers = [z_to(k) for k in (4, 3, 5, 2, 6, 1, 7)]
    peers += [x_to(k) for k in (2, 1, 3)]
    peers += [y_to(k) for k in (2, 1, 3)]
    peers += [sibling]
    for peer in peers:
        pl.semaphore_signal(barrier, inc=1, device_id=peer, device_id_type=pl.DeviceIdType.MESH)

    first = vecs.at[0]
    owner = jnp.minimum(z, 5)
    copies = [
        (right_hbm, right),
        (left_hbm, left),
        (psi.at[x, c, owner // 3, lax.rem(owner, 3)], fresh.at[0, owner // 3, lax.rem(owner, 3)]),
        (diagonal.at[x, c, owner // 3, lax.rem(owner, 3)], diagonal_own),
        (pair_in_hbm, pair_in),
        (pair_out_hbm, pair_out),
        (pair_count_hbm, pair_count),
    ]
    for cc in range(2):
        for b in range(3):
            copies.append((psi.at[:, cc, 0, b], first.at[cc, 0, b, :, y]))
            copies.append((psi.at[:, cc, 1, b], first.at[cc, 1, b, y]))
    loads = []
    for source, target in copies:
        load = pltpu.make_async_copy(source, target, load_sem.at[len(loads)])
        load.start()
        loads.append(load)

    def remote(source, target, send_sem, recv_sem, peer):
        return pltpu.make_async_remote_copy(
            src_ref=source,
            dst_ref=target,
            send_sem=send_sem,
            recv_sem=recv_sem,
            device_id=peer,
            device_id_type=pl.DeviceIdType.MESH,
        )

    def send(source, target, send_sem, recv_sem, peer):
        remote(source, target, send_sem, recv_sem, peer).start()

    def arrived(like, sem):
        remote(like, like, sem, sem, sibling).wait_recv()

    def left_here(like, sem):
        remote(like, like, sem, sem, sibling).wait_send()

    pl.semaphore_wait(barrier, len(peers))

    for k in (2, 1, 3):
        send(psi.at[x, c, 0], first.at[c, 0, :, x, y], near_s, near_r.at[k - 1], y_to(k))
    for b in range(3):
        for k in (2, 1, 3):
            send(psi.at[:, c, 1, b], first.at[c, 1, b, y], whole_s, whole_r.at[k - 1], y_to(k))

    loads[0].wait()

    def split_right(j, carry):
        high, low = halves(right[j].T)
        right3[j, 0:N] = high
        right3[j, N : 2 * N] = high
        right3[j, 2 * N :] = low
        return carry

    lax.fori_loop(0, 4, split_right, 0)

    def forward(k, carry):
        here = first.at[c, 0, :, x, lax.rem(y + 4 - k, 4)]
        arrived(here, near_r.at[k - 1])
        for m in (2, 1, 3):
            send(here, here, forward_s, forward_r.at[k - 1], x_to(m))
        return carry

    lax.fori_loop(1, 4, forward, 0)

    loads[1].wait()

    def split_left(j, carry):
        for cc in range(2):
            for xx in range(4):
                row = 96 * xx + 48 * cc
                high, low = halves(left[j, row : row + 48])
                rows = slice(48 * xx, 48 * xx + 48)
                left3[j, cc, rows, 0:N] = high
                left3[j, cc, rows, N : 2 * N] = high
                left3[j, cc, rows, 2 * N :] = low
        return carry

    lax.fori_loop(0, 4, split_left, 0)

    for load in loads[2:]:
        load.wait()

    def cross(k, carry):
        sector = lax.rem(y + 4 - k, 4)
        arrived(small_in.at[0, 0], forward_r.at[k - 1])
        here = first.at[c, 0, :, :, sector]
        send(here, here, cross_s.at[STEPS], cross_r.at[STEPS], sibling)
        arrived(big_in.at[0, 0, 0], whole_r.at[k - 1])
        here = first.at[c, 1, :, sector]
        send(here, here, cross_s.at[STEPS], cross_r.at[STEPS], sibling)
        return carry

    lax.fori_loop(1, 4, cross, 0)
    arrived(big_in.at[0], cross_r.at[STEPS])

    count = pair_count[0]
    live = [
        [jnp.logical_and(pair_out[0, j] == yy, count > j) for yy in range(4)] for j in range(4)
    ]

    def davidson_step(step, carry):
        vec = vecs.at[step]

        def convert(index, total):
            yy, xx = index // 4, lax.rem(index, 4)
            for cc in range(2):
                top = vec[cc, 0, :, xx, yy].reshape(24, N)
                bottom = vec[cc, 1, :, yy, xx].reshape(24, N)
                block = jnp.concatenate([top, bottom], axis=0)
                total = total + jnp.sum((block * block).reshape(6, 8, N), axis=0)
                high, low = halves(block)
                rows = pl.ds(pl.multiple_of(96 * xx + 48 * cc, 16), 48)
                vec3[yy, rows, 0:N] = high
                vec3[yy, rows, N : 2 * N] = low
                vec3[yy, rows, 2 * N :] = high
            return total

        squares = lax.fori_loop(0, 16, convert, jnp.zeros((8, N), F32))

        for j in range(4):
            high, low = halves(matmul(vec3[pair_in[0, j]], right3[j]))
            inner3[j, 0:N] = high
            inner3[j, N : 2 * N] = low
            inner3[j, 2 * N :] = high

        def combine(side, cls, b, store, dot):
            for xx in range(4):
                rows = pl.ds(pl.multiple_of(48 * xx + 24 * cls + 8 * b, 8), 8)
                blocks = [product[j, rows] for j in range(4)]
                for yy in range(4):
                    p, q = (xx, yy) if cls == 0 else (yy, xx)
                    terms = [jnp.where(live[j][yy], blocks[j], 0.0) for j in range(4)]
                    value = (terms[0] + terms[1]) + (terms[2] + terms[3])
                    store(p, q, value)
                    dot = dot + value * vec[side, cls, b, p, q]
            return dot

        far, own = part_far.at[step], part_near.at[step]
        for j in range(4):
            product[j] = matmul(left3[j, d], inner3[j])

        def far_rows(b, dot):
            for cls in range(2):

                def store(p, q, value, cls=cls):
                    far[cls, b, p, q] = value

                dot = combine(d, cls, b, store, dot)
                send(
                    far.at[cls, b],
                    core_in.at[step, cls, b],
                    core_s.at[step],
                    core_r.at[step, cls, b],
                    sibling,
                )
            return dot

        dot = lax.fori_loop(0, 3, far_rows, jnp.zeros((8, N), F32))
        for j in range(4):
            product[j] = matmul(left3[j, c], inner3[j])

        def near_rows(b, dot):
            for cls in range(2):
                arrived(core_in.at[step, cls, b], core_r.at[step, cls, b])

                def store(p, q, value, cls=cls):
                    own[cls, b, p, q] = value + core_in[step, cls, b, p, q]

                dot = combine(c, cls, b, store, dot)
            return dot

        def large(b):
            if b:
                left_here(big_in.at[0, :, 0], big_s.at[step, b - 1])
            for cls in range(2):
                for m in (2, 1, 3):
                    send(
                        own.at[cls, b, lax.rem(p_me[cls] + m, 4)],
                        big_in.at[step, cls, b, m - 1],
                        big_s.at[step, b],
                        big_r.at[step, cls, b],
                        p_to[cls](m),
                    )

        dot = near_rows(0, dot)
        large(0)
        dot = lax.fori_loop(1, 3, near_rows, dot)

        tiles = dots.at[step]
        tiles[c] = dot[:, 0:128] + dot[:, 128:256] + dot[:, 256:384]
        send(tiles.at[c], tiles.at[c], dot_s.at[step], dot_r.at[step, 0], sibling)
        arrived(tiles.at[0], dot_r.at[step, 0])
        tiles[2 + z] = tiles[0] + tiles[1]
        for k in (4, 3, 5, 2, 6, 1, 7):
            send(tiles.at[2 + z], tiles.at[2 + z], dot_s.at[step], dot_r.at[step, 1], z_to(k))

        mean_square = jnp.sum(squares, axis=(0, 1), keepdims=True) / CELLS + EPSILON
        inverse = 1.0 / jnp.sqrt(mean_square)

        def small(b):
            for cls in range(2):
                arrived(big_in.at[step, cls, b], big_r.at[step, cls, b])
                value = own[cls, b, p_me[cls]] + big_in[step, cls, b, 0]
                value = value + (big_in[step, cls, b, 1] + big_in[step, cls, b, 2])
                mid[step, cls, b] = value
                for k in (2, 1, 3):
                    send(
                        mid.at[step, cls, b, lax.rem(q_me[cls] + k, 4)],
                        small_in.at[step, cls, b, k - 1],
                        small_s.at[step],
                        small_r.at[step, cls, b],
                        q_to[cls](k),
                    )

        def to_owner(b):
            for cls in range(2):
                arrived(small_in.at[step, cls, b], small_r.at[step, cls, b])
                value = mid[step, cls, b, q_me[cls]] + small_in[step, cls, b, 0]
                last[step, cls, b] = value + (small_in[step, cls, b, 1] + small_in[step, cls, b, 2])
                to = 3 * cls + b

                @pl.when(z != to)
                def _(to=to, cls=cls):
                    send(
                        last.at[step, cls, b],
                        z_in.at[step, lax.rem(to - z + 8, 8) - 1],
                        z_s.at[step],
                        z_r.at[step],
                        device(to, x, c, y),
                    )

        def update(b, rayleigh):
            @pl.when(jnp.logical_or(z == b, z == b + 3))
            def _():
                high = z // 3
                normed = fresh[step, high, b] * inverse
                scale = 1.0 / jnp.maximum(jnp.abs(diagonal_own[...] - rayleigh), 1.0)
                arrived(z_in.at[step], z_r.at[step])
                total = last[step, high, b] + z_in[step, 6]
                for i in (0, 2, 4):
                    total = total + (z_in[step, i] + z_in[step, i + 1])
                residual = total * inverse - rayleigh * normed
                fresh[step + 1, high, b] = normed - residual * scale
                here = fresh.at[step + 1, high, b]
                for k in (4, 3, 5, 2, 6, 1, 7):
                    send(here, here, owner_s.at[step], owner_r.at[step, b], z_to(k))

        def from_owners(b):
            mine = jnp.logical_or(z == b, z == b + 3)

            @pl.when(mine)
            def _():
                arrived(z_in.at[step, pl.ds(0, 1)], owner_r.at[step, b])

            @pl.when(jnp.logical_not(mine))
            def _():
                arrived(z_in.at[step, pl.ds(0, 2)], owner_r.at[step, b])

        large(1)
        small(0)
        arrived(tiles.at[pl.ds(2, 7)], dot_r.at[step, 1])
        pairs = [tiles[2 + 2 * i] + tiles[3 + 2 * i] for i in range(4)]
        tiles[10 + x] = (pairs[0] + pairs[1]) + (pairs[2] + pairs[3])
        for k in (2, 1, 3):
            send(tiles.at[10 + x], tiles.at[10 + x], dot_s.at[step], dot_r.at[step, 2], x_to(k))
        large(2)
        small(1)
        to_owner(0)
        arrived(tiles.at[pl.ds(10, 3)], dot_r.at[step, 2])
        tiles[14 + y] = (tiles[10] + tiles[11]) + (tiles[12] + tiles[13])
        for k in (2, 1, 3):
            send(tiles.at[14 + y], tiles.at[14 + y], dot_s.at[step], dot_r.at[step, 3], y_to(k))
        small(2)
        to_owner(1)
        arrived(tiles.at[pl.ds(14, 3)], dot_r.at[step, 3])
        tile = (tiles[14] + tiles[15]) + (tiles[16] + tiles[17])
        rayleigh = jnp.sum(tile, axis=(0, 1), keepdims=True) * (inverse * inverse) / CELLS
        update(0, rayleigh)
        to_owner(2)
        energies[step] = jnp.sum(rayleigh)
        update(1, rayleigh)

        @pl.when(step < STEPS - 1)
        def _():
            after = vecs.at[step + 1]

            def grow(b):
                from_owners(b)
                for cls in range(2):
                    here = fresh.at[step + 1, cls, b]
                    there = after.at[c, cls, b, p_me[cls], q_me[cls]]
                    for k in (2, 1, 3):
                        send(here, there, grow_s, grow_r.at[cls, b], q_to[cls](k))
                    after[c, cls, b, p_me[cls], q_me[cls]] = fresh[step + 1, cls, b]

            def wide(b):
                for cls in range(2):
                    arrived(small_in.at[0, 0, 0], grow_r.at[cls, b])
                    here = after.at[c, cls, b, p_me[cls]]
                    for m in (2, 1, 3):
                        send(here, here, wide_s.at[b], wide_r.at[cls, b], p_to[cls](m))

            def over(b):
                for cls in range(2):
                    arrived(big_in.at[0, 0, 0], wide_r.at[cls, b])
                    here = after.at[c, cls, b]
                    send(here, here, cross_s.at[step], cross_r.at[step], sibling)

            grow(0)
            update(2, rayleigh)
            grow(1)
            wide(0)
            grow(2)
            wide(1)
            wide(2)
            over(0)
            over(1)
            over(2)
            arrived(after.at[d], cross_r.at[step])
            left_here(small_in.at[0], grow_s)
            for b in range(3):
                left_here(big_in.at[0, :, 0], wide_s.at[b])
            left_here(after.at[d], cross_s.at[step])

        @pl.when(step == STEPS - 1)
        def _():
            def grow(b):
                from_owners(b)
                here, there = fresh.at[step + 1, :, b], out.at[x, c, :, b]
                for m in (2, 1, 3):
                    send(here, there, end_s, end_r.at[b], x_to(m))
                out[x, c, :, b] = fresh[step + 1, :, b]

            def over(b):
                arrived(small_in.at[0, 0, pl.ds(0, 2)], end_r.at[b])
                here = out.at[:, c, :, b]
                send(here, here, cross_s.at[step], cross_r.at[step], sibling)

            grow(0)
            update(2, rayleigh)
            grow(1)
            over(0)
            grow(2)
            over(1)
            over(2)
            arrived(out.at[:, d], cross_r.at[step])
            left_here(small_in.at[0], end_s)
            left_here(out.at[:, d], cross_s.at[step])

        left_here(part_far.at[0], core_s.at[step])
        left_here(big_in.at[0, :, 0], big_s.at[step, 2])
        left_here(small_in.at[0], small_s.at[step])
        left_here(tiles.at[pl.ds(0, 14)], dot_s.at[step])

        @pl.when(z < 6)
        def _():
            left_here(z_in.at[step, pl.ds(0, 5)], z_s.at[step])
            left_here(z_in.at[step], owner_s.at[step])

        @pl.when(z >= 6)
        def _():
            left_here(z_in.at[step, pl.ds(0, 6)], z_s.at[step])

        return carry

    lax.fori_loop(0, STEPS, davidson_step, 0)

    left_here(small_in.at[0, 0], near_s)
    left_here(big_in.at[0, 0], whole_s)
    left_here(part_far.at[0, 0, :, pl.ds(0, 3), pl.ds(0, 3)], forward_s)
    left_here(big_in.at[0], cross_s.at[STEPS])


def shards(psi_start, diagonal, left_ops, right_ops, pair_in, pair_out, pair_count):
    vmem = pl.BlockSpec(memory_space=pltpu.VMEM)
    smem = pl.BlockSpec(memory_space=pltpu.SMEM)
    hbm = pl.BlockSpec(memory_space=pltpu.HBM)
    dma = pltpu.SemaphoreType.DMA
    rows = (3, 8, N)
    blocks = (4, 2, 2, *rows)
    pieces = (2, 3, 4, 4, 8, N)
    psi, energies = pl.pallas_call(
        kernel,
        out_shape=(
            jax.ShapeDtypeStruct(blocks, F32),
            jax.ShapeDtypeStruct((STEPS,), F32),
        ),
        in_specs=[hbm] * 7,
        out_specs=(vmem, smem),
        scratch_shapes=[
            pltpu.SMEM((1, 4), jnp.int32),
            pltpu.SMEM((1, 4), jnp.int32),
            pltpu.SMEM((1,), jnp.int32),
            pltpu.VMEM((8, N), F32),
            pltpu.VMEM((4, N, N), F32),
            pltpu.VMEM((4, N, N), F32),
            pltpu.VMEM((4, 2, N // 2, 3 * N), BF16),
            pltpu.VMEM((4, 3 * N, N), BF16),
            pltpu.VMEM((4, N, 3 * N), BF16),
            pltpu.VMEM((4, 3 * N, N), BF16),
            pltpu.VMEM((4, N // 2, N), F32),
            pltpu.VMEM((STEPS, 2, *pieces), F32),
            pltpu.VMEM((STEPS, *pieces), F32),
            pltpu.VMEM((STEPS, *pieces), F32),
            pltpu.VMEM((STEPS, *pieces), F32),
            pltpu.VMEM((STEPS, 2, 3, 3, 4, 8, N), F32),
            pltpu.VMEM((STEPS, 2, 3, 4, 8, N), F32),
            pltpu.VMEM((STEPS, 2, 3, 3, 8, N), F32),
            pltpu.VMEM((STEPS, 2, *rows), F32),
            pltpu.VMEM((STEPS, 7, 8, N), F32),
            pltpu.VMEM((STEPS + 1, 2, *rows), F32),
            pltpu.VMEM((STEPS, 18, 8, 128), F32),
            dma((19,)),
            dma,
            dma((3,)),
            dma,
            dma((3,)),
            dma,
            dma((3,)),
            dma((STEPS,)),
            dma((STEPS, 2, 3)),
            dma((STEPS, 3)),
            dma((STEPS, 2, 3)),
            dma((STEPS,)),
            dma((STEPS, 2, 3)),
            dma((STEPS,)),
            dma((STEPS,)),
            dma((STEPS,)),
            dma((STEPS, 3)),
            dma,
            dma((2, 3)),
            dma((3,)),
            dma((2, 3)),
            dma((STEPS + 1,)),
            dma((STEPS + 1,)),
            dma,
            dma((3,)),
            dma((STEPS,)),
            dma((STEPS, 4)),
        ],
        compiler_params=pltpu.CompilerParams(
            collective_id=0, has_side_effects=True, vmem_limit_bytes=54400 * 1024
        ),
    )(
        pltpu.with_memory_space_constraint(pair_in, pltpu.HBM),
        pltpu.with_memory_space_constraint(pair_out, pltpu.HBM),
        pair_count,
        psi_start.reshape(blocks),
        diagonal.reshape(blocks),
        left_ops,
        right_ops,
    )
    return psi.reshape(1, N, N), energies


def solution(mesh):
    both = ("term", "sector")
    in_specs = (
        P("sector", None, None),
        P("sector", None, None),
        P(both, None, None),
        P(both, None, None),
        P(both, None),
        P(both, None),
        P(both),
    )
    out_specs = (P("sector", None, None), P())
    return jax.shard_map(
        shards, mesh=mesh, in_specs=in_specs, out_specs=out_specs, check_vma=False
    )
```

```python
import functools

import jax
import jax.numpy as jnp
from jax import lax
from jax.experimental import pallas as pl
from jax.experimental.pallas import tpu as pltpu
from jax.sharding import PartitionSpec as P

STEPS = 2
EPSILON = 1e-06
N = 384
CELLS = float(4 * N * N)
F32 = jnp.float32
BF16 = jnp.bfloat16


def matmul(a, b):
    return lax.dot_general(a, b, (((1,), (0,)), ((), ())), preferred_element_type=F32)


def halves(value):
    high = value.astype(BF16)
    return high, (value - high.astype(F32)).astype(BF16)


def kernel(
    pair_in_hbm,
    pair_out_hbm,
    pair_count_hbm,
    psi,
    diagonal,
    left_hbm,
    right_hbm,
    out,
    energies,
    pair_in,
    pair_out,
    pair_count,
    diagonal_own,
    left,
    right,
    left3,
    right3,
    vec3,
    inner3,
    product,
    vecs,
    part_far,
    part_near,
    core_in,
    big_in,
    mid,
    small_in,
    last,
    z_in,
    fresh,
    dots,
    load_sem,
    near_s,
    near_r,
    whole_s,
    whole_r,
    forward_s,
    forward_r,
    core_s,
    core_r,
    big_s,
    big_r,
    small_s,
    small_r,
    z_s,
    z_r,
    owner_s,
    owner_r,
    grow_s,
    grow_r,
    wide_s,
    wide_r,
    cross_s,
    cross_r,
    end_s,
    end_r,
    dot_s,
    dot_r,
):
    t = lax.axis_index("term")
    y = lax.axis_index("sector")
    z = t // 8
    x = lax.rem(t // 2, 4)
    c = lax.rem(t, 2)
    d = 1 - c

    def device(z_, x_, c_, y_):
        return ((z_ * 4 + x_) * 2 + c_, y_)

    def x_to(k):
        return device(z, lax.rem(x + k, 4), c, y)

    def y_to(k):
        return device(z, x, c, lax.rem(y + k, 4))

    def z_to(k):
        return device(lax.rem(z + k, 8), x, c, y)

    sibling = device(z, x, d, y)

    p_me, q_me = (x, y), (y, x)
    p_to, q_to = (x_to, y_to), (y_to, x_to)

    barrier = pltpu.get_barrier_semaphore()
    peers = [z_to(k) for k in (4, 3, 5, 2, 6, 1, 7)]
    peers += [x_to(k) for k in (2, 1, 3)]
    peers += [y_to(k) for k in (2, 1, 3)]
    peers += [sibling]
    for peer in peers:
        pl.semaphore_signal(barrier, inc=1, device_id=peer, device_id_type=pl.DeviceIdType.MESH)

    first = vecs.at[0]
    owner = jnp.minimum(z, 5)
    copies = [
        (right_hbm, right),
        (left_hbm, left),
        (psi.at[x, c, owner // 3, lax.rem(owner, 3)], fresh.at[0, owner // 3, lax.rem(owner, 3)]),
        (diagonal.at[x, c, owner // 3, lax.rem(owner, 3)], diagonal_own),
        (pair_in_hbm, pair_in),
        (pair_out_hbm, pair_out),
        (pair_count_hbm, pair_count),
    ]
    for cc in range(2):
        for b in range(3):
            copies.append((psi.at[:, cc, 0, b], first.at[cc, 0, b, :, y]))
            copies.append((psi.at[:, cc, 1, b], first.at[cc, 1, b, y]))
    loads = []
    for source, target in copies:
        load = pltpu.make_async_copy(source, target, load_sem.at[len(loads)])
        load.start()
        loads.append(load)

    def remote(source, target, send_sem, recv_sem, peer):
        return pltpu.make_async_remote_copy(
            src_ref=source,
            dst_ref=target,
            send_sem=send_sem,
            recv_sem=recv_sem,
            device_id=peer,
            device_id_type=pl.DeviceIdType.MESH,
        )

    def send(source, target, send_sem, recv_sem, peer):
        remote(source, target, send_sem, recv_sem, peer).start()

    def arrived(like, sem):
        remote(like, like, sem, sem, sibling).wait_recv()

    def left_here(like, sem):
        remote(like, like, sem, sem, sibling).wait_send()

    pl.semaphore_wait(barrier, len(peers))

    for k in (2, 1, 3):
        send(psi.at[x, c, 0], first.at[c, 0, :, x, y], near_s, near_r.at[k - 1], y_to(k))
    for b in range(3):
        for k in (2, 1, 3):
            send(psi.at[:, c, 1, b], first.at[c, 1, b, y], whole_s, whole_r.at[k - 1], y_to(k))

    loads[0].wait()

    def split_right(j, carry):
        high, low = halves(right[j].T)
        right3[j, 0:N] = high
        right3[j, N : 2 * N] = high
        right3[j, 2 * N :] = low
        return carry

    lax.fori_loop(0, 4, split_right, 0)

    def forward(i, carry):
        k = lax.rem(2 * i, 3) + 1
        here = first.at[c, 0, :, x, lax.rem(y + 4 - k, 4)]
        arrived(here, near_r.at[k - 1])
        for m in (2, 1, 3):
            send(here, here, forward_s, forward_r.at[k - 1], x_to(m))
        return carry

    lax.fori_loop(0, 3, forward, 0)

    loads[1].wait()

    def split_left(j, carry):
        for cc in range(2):
            for xx in range(4):
                row = 96 * xx + 48 * cc
                high, low = halves(left[j, row : row + 48])
                rows = slice(48 * xx, 48 * xx + 48)
                left3[j, cc, rows, 0:N] = high
                left3[j, cc, rows, N : 2 * N] = high
                left3[j, cc, rows, 2 * N :] = low
        return carry

    lax.fori_loop(0, 4, split_left, 0)

    for load in loads[2:]:
        load.wait()

    def cross(i, carry):
        k = lax.rem(2 * i, 3) + 1
        sector = lax.rem(y + 4 - k, 4)
        arrived(small_in.at[0, 0], forward_r.at[k - 1])
        here = first.at[c, 0, :, :, sector]
        send(here, here, cross_s.at[STEPS], cross_r.at[STEPS], sibling)
        arrived(big_in.at[0, 0, 0], whole_r.at[k - 1])
        here = first.at[c, 1, :, sector]
        send(here, here, cross_s.at[STEPS], cross_r.at[STEPS], sibling)
        return carry

    lax.fori_loop(0, 3, cross, 0)
    arrived(big_in.at[0], cross_r.at[STEPS])

    count = pair_count[0]
    live = [
        [jnp.logical_and(pair_out[0, j] == yy, count > j) for yy in range(4)] for j in range(4)
    ]

    def davidson_step(step, carry):
        vec = vecs.at[step]

        def convert(index, total):
            yy, xx = index // 4, lax.rem(index, 4)
            for cc in range(2):
                top = vec[cc, 0, :, xx, yy].reshape(24, N)
                bottom = vec[cc, 1, :, yy, xx].reshape(24, N)
                block = jnp.concatenate([top, bottom], axis=0)
                total = total + jnp.sum((block * block).reshape(6, 8, N), axis=0)
                high, low = halves(block)
                rows = pl.ds(pl.multiple_of(96 * xx + 48 * cc, 16), 48)
                vec3[yy, rows, 0:N] = high
                vec3[yy, rows, N : 2 * N] = low
                vec3[yy, rows, 2 * N :] = high
            return total

        squares = lax.fori_loop(0, 16, convert, jnp.zeros((8, N), F32))

        for j in range(4):
            high, low = halves(matmul(vec3[pair_in[0, j]], right3[j]))
            inner3[j, 0:N] = high
            inner3[j, N : 2 * N] = low
            inner3[j, 2 * N :] = high

        def combine(side, cls, b, store, dot):
            for xx in range(4):
                rows = pl.ds(pl.multiple_of(48 * xx + 24 * cls + 8 * b, 8), 8)
                blocks = [product[j, rows] for j in range(4)]
                for yy in range(4):
                    p, q = (xx, yy) if cls == 0 else (yy, xx)
                    terms = [jnp.where(live[j][yy], blocks[j], 0.0) for j in range(4)]
                    value = (terms[0] + terms[1]) + (terms[2] + terms[3])
                    store(p, q, value)
                    dot = dot + value * vec[side, cls, b, p, q]
            return dot

        far, own = part_far.at[step], part_near.at[step]
        for j in range(4):
            product[j] = matmul(left3[j, d], inner3[j])

        def far_rows(b, dot):
            for cls in range(2):

                def store(p, q, value, cls=cls):
                    far[cls, b, p, q] = value

                dot = combine(d, cls, b, store, dot)
                send(
                    far.at[cls, b],
                    core_in.at[step, cls, b],
                    core_s.at[step],
                    core_r.at[step, cls, b],
                    sibling,
                )
            return dot

        dot = lax.fori_loop(0, 3, far_rows, jnp.zeros((8, N), F32))
        for j in range(4):
            product[j] = matmul(left3[j, c], inner3[j])

        def near_rows(b, dot):
            for cls in range(2):
                arrived(core_in.at[step, cls, b], core_r.at[step, cls, b])

                def store(p, q, value, cls=cls):
                    own[cls, b, p, q] = value + core_in[step, cls, b, p, q]

                dot = combine(c, cls, b, store, dot)
            return dot

        def large(b):
            if b:
                left_here(big_in.at[0, :, 0], big_s.at[step, b - 1])
            for cls in range(2):
                for m in (2, 1, 3):
                    send(
                        own.at[cls, b, lax.rem(p_me[cls] + m, 4)],
                        big_in.at[step, cls, b, m - 1],
                        big_s.at[step, b],
                        big_r.at[step, cls, b],
                        p_to[cls](m),
                    )

        dot = near_rows(0, dot)
        large(0)
        dot = lax.fori_loop(1, 3, near_rows, dot)

        tiles = dots.at[step]
        tiles[c] = dot[:, 0:128] + dot[:, 128:256] + dot[:, 256:384]
        send(tiles.at[c], tiles.at[c], dot_s.at[step], dot_r.at[step, 0], sibling)
        arrived(tiles.at[0], dot_r.at[step, 0])
        tiles[2 + z] = tiles[0] + tiles[1]
        for k in (4, 3, 5, 2, 6, 1, 7):
            send(tiles.at[2 + z], tiles.at[2 + z], dot_s.at[step], dot_r.at[step, 1], z_to(k))

        mean_square = jnp.sum(squares, axis=(0, 1), keepdims=True) / CELLS + EPSILON
        inverse = 1.0 / jnp.sqrt(mean_square)

        def small(b):
            for cls in range(2):
                arrived(big_in.at[step, cls, b], big_r.at[step, cls, b])
                value = own[cls, b, p_me[cls]] + big_in[step, cls, b, 0]
                value = value + (big_in[step, cls, b, 1] + big_in[step, cls, b, 2])
                mid[step, cls, b] = value
                for k in (2, 1, 3):
                    send(
                        mid.at[step, cls, b, lax.rem(q_me[cls] + k, 4)],
                        small_in.at[step, cls, b, k - 1],
                        small_s.at[step],
                        small_r.at[step, cls, b],
                        q_to[cls](k),
                    )

        def to_owner(b):
            for cls in range(2):
                arrived(small_in.at[step, cls, b], small_r.at[step, cls, b])
                value = mid[step, cls, b, q_me[cls]] + small_in[step, cls, b, 0]
                last[step, cls, b] = value + (small_in[step, cls, b, 1] + small_in[step, cls, b, 2])
                to = 3 * cls + b

                @pl.when(z != to)
                def _(to=to, cls=cls):
                    send(
                        last.at[step, cls, b],
                        z_in.at[step, lax.rem(to - z + 8, 8) - 1],
                        z_s.at[step],
                        z_r.at[step],
                        device(to, x, c, y),
                    )

        def update(b, rayleigh):
            @pl.when(jnp.logical_or(z == b, z == b + 3))
            def _():
                high = z // 3
                normed = fresh[step, high, b] * inverse
                scale = 1.0 / jnp.maximum(jnp.abs(diagonal_own[...] - rayleigh), 1.0)
                arrived(z_in.at[step], z_r.at[step])
                total = last[step, high, b] + z_in[step, 6]
                for i in (0, 2, 4):
                    total = total + (z_in[step, i] + z_in[step, i + 1])
                residual = total * inverse - rayleigh * normed
                fresh[step + 1, high, b] = normed - residual * scale
                here = fresh.at[step + 1, high, b]
                for k in (4, 3, 5, 2, 6, 1, 7):
                    send(here, here, owner_s.at[step], owner_r.at[step, b], z_to(k))

        def from_owners(b):
            mine = jnp.logical_or(z == b, z == b + 3)

            @pl.when(mine)
            def _():
                arrived(z_in.at[step, pl.ds(0, 1)], owner_r.at[step, b])

            @pl.when(jnp.logical_not(mine))
            def _():
                arrived(z_in.at[step, pl.ds(0, 2)], owner_r.at[step, b])

        large(1)
        small(0)
        arrived(tiles.at[pl.ds(2, 7)], dot_r.at[step, 1])
        pairs = [tiles[2 + 2 * i] + tiles[3 + 2 * i] for i in range(4)]
        tiles[10 + x] = (pairs[0] + pairs[1]) + (pairs[2] + pairs[3])
        for k in (2, 1, 3):
            send(tiles.at[10 + x], tiles.at[10 + x], dot_s.at[step], dot_r.at[step, 2], x_to(k))
        large(2)
        small(1)
        to_owner(0)
        arrived(tiles.at[pl.ds(10, 3)], dot_r.at[step, 2])
        tiles[14 + y] = (tiles[10] + tiles[11]) + (tiles[12] + tiles[13])
        for k in (2, 1, 3):
            send(tiles.at[14 + y], tiles.at[14 + y], dot_s.at[step], dot_r.at[step, 3], y_to(k))
        small(2)
        to_owner(1)
        arrived(tiles.at[pl.ds(14, 3)], dot_r.at[step, 3])
        tile = (tiles[14] + tiles[15]) + (tiles[16] + tiles[17])
        rayleigh = jnp.sum(tile, axis=(0, 1), keepdims=True) * (inverse * inverse) / CELLS
        update(0, rayleigh)
        to_owner(2)
        energies[step] = jnp.sum(rayleigh)
        update(1, rayleigh)

        @pl.when(step < STEPS - 1)
        def _():
            after = vecs.at[step + 1]

            def grow(b):
                from_owners(b)
                for cls in range(2):
                    here = fresh.at[step + 1, cls, b]
                    there = after.at[c, cls, b, p_me[cls], q_me[cls]]
                    for k in (2, 1, 3):
                        send(here, there, grow_s, grow_r.at[cls, b], q_to[cls](k))
                    after[c, cls, b, p_me[cls], q_me[cls]] = fresh[step + 1, cls, b]

            def wide(b):
                for cls in range(2):
                    arrived(small_in.at[0, 0, 0], grow_r.at[cls, b])
                    here = after.at[c, cls, b, p_me[cls]]
                    for m in (2, 1, 3):
                        send(here, here, wide_s.at[b], wide_r.at[cls, b], p_to[cls](m))

            def over(b):
                for cls in range(2):
                    arrived(big_in.at[0, 0, 0], wide_r.at[cls, b])
                    here = after.at[c, cls, b]
                    send(here, here, cross_s.at[step], cross_r.at[step], sibling)

            grow(0)
            update(2, rayleigh)
            grow(1)
            wide(0)
            grow(2)
            wide(1)
            wide(2)
            over(0)
            over(1)
            over(2)
            arrived(after.at[d], cross_r.at[step])
            left_here(small_in.at[0], grow_s)
            for b in range(3):
                left_here(big_in.at[0, :, 0], wide_s.at[b])
            left_here(after.at[d], cross_s.at[step])

        @pl.when(step == STEPS - 1)
        def _():
            def grow(b):
                from_owners(b)
                here, there = fresh.at[step + 1, :, b], out.at[x, c, :, b]
                for m in (2, 1, 3):
                    send(here, there, end_s, end_r.at[b], x_to(m))
                out[x, c, :, b] = fresh[step + 1, :, b]

            def over(b):
                arrived(small_in.at[0, 0, pl.ds(0, 2)], end_r.at[b])
                here = out.at[:, c, :, b]
                send(here, here, cross_s.at[step], cross_r.at[step], sibling)

            grow(0)
            update(2, rayleigh)
            grow(1)
            over(0)
            grow(2)
            over(1)
            over(2)
            arrived(out.at[:, d], cross_r.at[step])
            left_here(small_in.at[0], end_s)
            left_here(out.at[:, d], cross_s.at[step])

        left_here(part_far.at[0], core_s.at[step])
        left_here(big_in.at[0, :, 0], big_s.at[step, 2])
        left_here(small_in.at[0], small_s.at[step])
        left_here(tiles.at[pl.ds(0, 14)], dot_s.at[step])

        @pl.when(z < 6)
        def _():
            left_here(z_in.at[step, pl.ds(0, 5)], z_s.at[step])
            left_here(z_in.at[step], owner_s.at[step])

        @pl.when(z >= 6)
        def _():
            left_here(z_in.at[step, pl.ds(0, 6)], z_s.at[step])

        return carry

    lax.fori_loop(0, STEPS, davidson_step, 0)

    left_here(small_in.at[0, 0], near_s)
    left_here(big_in.at[0, 0], whole_s)
    left_here(part_far.at[0, 0, :, pl.ds(0, 3), pl.ds(0, 3)], forward_s)
    left_here(big_in.at[0], cross_s.at[STEPS])


def shards(psi_start, diagonal, left_ops, right_ops, pair_in, pair_out, pair_count):
    vmem = pl.BlockSpec(memory_space=pltpu.VMEM)
    smem = pl.BlockSpec(memory_space=pltpu.SMEM)
    hbm = pl.BlockSpec(memory_space=pltpu.HBM)
    dma = pltpu.SemaphoreType.DMA
    rows = (3, 8, N)
    blocks = (4, 2, 2, *rows)
    pieces = (2, 3, 4, 4, 8, N)
    psi, energies = pl.pallas_call(
        kernel,
        out_shape=(
            jax.ShapeDtypeStruct(blocks, F32),
            jax.ShapeDtypeStruct((STEPS,), F32),
        ),
        in_specs=[hbm] * 7,
        out_specs=(vmem, smem),
        scratch_shapes=[
            pltpu.SMEM((1, 4), jnp.int32),
            pltpu.SMEM((1, 4), jnp.int32),
            pltpu.SMEM((1,), jnp.int32),
            pltpu.VMEM((8, N), F32),
            pltpu.VMEM((4, N, N), F32),
            pltpu.VMEM((4, N, N), F32),
            pltpu.VMEM((4, 2, N // 2, 3 * N), BF16),
            pltpu.VMEM((4, 3 * N, N), BF16),
            pltpu.VMEM((4, N, 3 * N), BF16),
            pltpu.VMEM((4, 3 * N, N), BF16),
            pltpu.VMEM((4, N // 2, N), F32),
            pltpu.VMEM((STEPS, 2, *pieces), F32),
            pltpu.VMEM((STEPS, *pieces), F32),
            pltpu.VMEM((STEPS, *pieces), F32),
            pltpu.VMEM((STEPS, *pieces), F32),
            pltpu.VMEM((STEPS, 2, 3, 3, 4, 8, N), F32),
            pltpu.VMEM((STEPS, 2, 3, 4, 8, N), F32),
            pltpu.VMEM((STEPS, 2, 3, 3, 8, N), F32),
            pltpu.VMEM((STEPS, 2, *rows), F32),
            pltpu.VMEM((STEPS, 7, 8, N), F32),
            pltpu.VMEM((STEPS + 1, 2, *rows), F32),
            pltpu.VMEM((STEPS, 18, 8, 128), F32),
            dma((19,)),
            dma,
            dma((3,)),
            dma,
            dma((3,)),
            dma,
            dma((3,)),
            dma((STEPS,)),
            dma((STEPS, 2, 3)),
            dma((STEPS, 3)),
            dma((STEPS, 2, 3)),
            dma((STEPS,)),
            dma((STEPS, 2, 3)),
            dma((STEPS,)),
            dma((STEPS,)),
            dma((STEPS,)),
            dma((STEPS, 3)),
            dma,
            dma((2, 3)),
            dma((3,)),
            dma((2, 3)),
            dma((STEPS + 1,)),
            dma((STEPS + 1,)),
            dma,
            dma((3,)),
            dma((STEPS,)),
            dma((STEPS, 4)),
        ],
        compiler_params=pltpu.CompilerParams(
            collective_id=0, has_side_effects=True, vmem_limit_bytes=54400 * 1024
        ),
    )(
        pltpu.with_memory_space_constraint(pair_in, pltpu.HBM),
        pltpu.with_memory_space_constraint(pair_out, pltpu.HBM),
        pair_count,
        psi_start.reshape(blocks),
        diagonal.reshape(blocks),
        left_ops,
        right_ops,
    )
    return psi.reshape(1, N, N), energies


def solution(mesh):
    both = ("term", "sector")
    in_specs = (
        P("sector", None, None),
        P("sector", None, None),
        P(both, None, None),
        P(both, None, None),
        P(both, None),
        P(both, None),
        P(both),
    )
    out_specs = (P("sector", None, None), P())
    return jax.shard_map(
        shards, mesh=mesh, in_specs=in_specs, out_specs=out_specs, check_vma=False
    )
```
